256 devices in a mesh: dp: 16 (over z, core), tensor: 16 (over x, y).
Axes of the slice: x: 4, y: 4, z: 8, core: 2. Of those that a mesh axis runs over, the one named last changes fastest.
Arguments:
- grad_kv: bfloat16 [16, 8192, 2048], P('dp', None, 'tensor'), may hold values from -6 to 6
- error_kv: bfloat16 [16, 8192, 2048], P('dp', None, 'tensor'), may hold values from -6 to 6
- grad_out: bfloat16 [16, 4096, 4096], P('dp', 'tensor'), may hold values from -6 to 6
- error_out: bfloat16 [16, 4096, 4096], P('dp', 'tensor'), may hold values from -6 to 6
- warm_kv: float32 [2048, 8], P('tensor'), may hold values from -6 to 6
- warm_out: float32 [4096, 8], replicated, may hold values from -6 to 6
Outputs:
- factor_kv: float32 [2048, 8], P('tensor')
- factor_out: float32 [4096, 8], replicated
- residual_kv: bfloat16 [16, 8192, 2048], P('dp', None, 'tensor')
- residual_out: bfloat16 [16, 4096, 4096], P('dp', 'tensor')
The draws below stay inside these ranges and needn't reach their ends.
All inputs are finite; a program needn't handle non-finite values.
Results may differ from the reference program's by a relative error of at most 0.012.
Values sent between devices are 32-bit elements; how exact they have to be, the bound alone decides.
No kernel may reach another device: no remote copies, remote signals or barrier semaphores. Data moves between devices by JAX's collectives and lax.ppermute only.
A program may use at most 64 MiB of HBM per device.

```python
import jax
import jax.numpy as jnp
from jax import lax

D = 8192
KVW = 2048
OIN = 4096
OOUT = 4096
RANK = 8
N_DP = 16


def level_of(key, extent, split, least, high):
    def one(dim, shards_of):
        heights = jax.random.uniform(jax.random.fold_in(jax.random.fold_in(key, 6), dim), (shards_of,), jnp.float32, least / len(split), high / len(split))
        return jnp.repeat(jnp.exp(heights), extent[dim] // shards_of).reshape((-1,) + (1,) * (len(extent) - dim - 1))

    gain = one(*split[0])
    for cut in split[1:]:
        gain = gain * one(*cut)
    return gain


def centred(rng, extent, width, most, pieces=(), held_as=jnp.bfloat16):
    drawn = jax.random.normal(rng, extent, jnp.float32) * width
    if len(pieces) > 0:
        drawn = level_of(rng, extent, pieces, -0.22, 0.18) * drawn
    return jnp.clip(drawn, min=-most, max=most).astype(held_as)


def setup_inputs(seed: int = 0) -> dict:
    seeds = jax.random.split(jax.random.key(seed), 7)
    return {
        "grad_kv": centred(seeds[0], (N_DP, D, KVW), 1.0, 6.0, ((0, 16), (2, 16))),
        "error_kv": centred(seeds[1], (N_DP, D, KVW), 0.5, 6.0, ((0, 16), (2, 16))),
        "grad_out": centred(seeds[2], (N_DP, OIN, OOUT), 1.0, 6.0, ((0, 16), (1, 16))),
        "error_out": centred(seeds[3], (N_DP, OIN, OOUT), 0.5, 6.0, ((0, 16), (1, 16))),
        "warm_kv": centred(seeds[4], (KVW, RANK), 1.0, 6.0, ((0, 16),), jnp.float32),
        "warm_out": centred(seeds[5], (OOUT, RANK), 1.0, 6.0, (), jnp.float32),
    }


def merge_pair(pair):
    return (pair[0].astype(jnp.float32) + pair[1].astype(jnp.float32)).astype(jnp.bfloat16)

def orthonormal(sketch):
    gram = jnp.dot(sketch.T.astype(jnp.float32), sketch.astype(jnp.float32), precision=lax.Precision.HIGHEST, preferred_element_type=jnp.float32)
    gram = gram + 1e-06 * jnp.eye(gram.shape[0], dtype=jnp.float32)
    lower = jnp.linalg.cholesky(gram)
    return jax.scipy.linalg.solve_triangular(lower, sketch.T, lower=True).T

def compress(grads, errors, warm):
    initial = warm.astype(jnp.bfloat16)
    sketch = jnp.sum(lax.map(lambda pair: jnp.dot(merge_pair(pair).astype(jnp.float32), initial.astype(jnp.float32), preferred_element_type=jnp.float32), (grads, errors)), axis=0)
    basis = orthonormal(sketch)
    low = basis.astype(jnp.bfloat16)
    factor = jnp.sum(lax.map(lambda pair: jnp.dot(merge_pair(pair).T.astype(jnp.float32), low.astype(jnp.float32), preferred_element_type=jnp.float32), (grads, errors)), axis=0) / N_DP
    approx = jnp.dot(basis.astype(jnp.float32), factor.T.astype(jnp.float32), precision=lax.Precision.HIGHEST, preferred_element_type=jnp.float32)
    residual = lax.map(lambda pair: (merge_pair(pair).astype(jnp.float32) - approx).astype(jnp.bfloat16), (grads, errors))
    return (factor, residual)

def reference(grad_kv, error_kv, grad_out, error_out, warm_kv, warm_out):
    factor_kv, residual_kv = compress(grad_kv, error_kv, warm_kv)
    factor_out, residual_out = compress(grad_out, error_out, warm_out)
    return (factor_kv, factor_out, residual_kv, residual_out)
```

```python
import jax
import jax.numpy as jnp
from jax import lax
from jax.experimental import pallas as pl
from jax.experimental.pallas import tpu as pltpu
from jax.sharding import PartitionSpec as P

epsilon = 1e-06
f32 = jnp.float32
bf16 = jnp.bfloat16
LANES = 128
KV_CHUNKS = 8
OUT_CHUNKS = 8
limit = pltpu.CompilerParams(vmem_limit_bytes=24 * 1024 * 1024)
whole = pl.BlockSpec(memory_space=pltpu.VMEM)


def resident(value):
    return pltpu.with_memory_space_constraint(value, pltpu.VMEM)


def distant(value):
    return pltpu.with_memory_space_constraint(value, pltpu.HBM)


def merge(grad, error):
    return (grad.astype(f32) + error.astype(f32)).astype(bf16)


def split(value):
    high = value.astype(bf16)
    low = (value - high.astype(f32)).astype(bf16)
    return high, low


def row(tile, index):
    return jnp.broadcast_to(tile[index : index + 1, :], tile.shape)


def gram_columns(tiles):
    sums = [None] * 8
    for tile in tiles:
        for j in range(8):
            product = tile * row(tile, j)
            sums[j] = product if sums[j] is None else sums[j] + product
    return [
        jnp.broadcast_to(jnp.sum(total, axis=1, keepdims=True), (8, LANES)) for total in sums
    ]


def cholesky(columns):
    place = lax.broadcasted_iota(jnp.int32, (8, LANES), 0)
    columns = [
        column + jnp.where(place == j, epsilon, 0.0).astype(f32)
        for j, column in enumerate(columns)
    ]
    steps = []
    scale = jnp.zeros((8, LANES), f32)
    for j in range(8):
        inverse = lax.rsqrt(jnp.maximum(row(columns[j], j), epsilon))
        lower = jnp.where(place > j, columns[j] * inverse, 0.0)
        for k in range(j + 1, 8):
            columns[k] = columns[k] - lower * row(lower, k)
        steps.append(lower * inverse)
        scale = jnp.where(place == j, inverse, scale)
    return steps, scale


def substitute(tile, steps, scale):
    for j in range(7):
        tile = tile - steps[j] * row(tile, j)
    return tile * scale


def left_terms(value):
    high, low = split(value)
    high, low = high.astype(f32), low.astype(f32)
    return jnp.concatenate([high, low, high, jnp.zeros_like(high)], axis=0).T.astype(bf16)


def right_terms(value):
    high, low = split(value)
    high, low = high.astype(f32), low.astype(f32)
    return jnp.concatenate([high, high, low, jnp.zeros_like(high)], axis=0).astype(bf16)


def first(core, grad_kv, error_kv, grad_out, error_out, warm_kv, warm_out, merged_kv, merged_out,
          keep, give, gkv, ekv, gout, eout, arrived):
    rows = gkv.shape[0] // KV_CHUNKS
    wide = gout.shape[1] // OUT_CHUNKS
    copies = []
    for c in range(KV_CHUNKS):
        part = pl.ds(c * rows, rows)
        for k, (source, target) in enumerate(((grad_kv, gkv), (error_kv, ekv))):
            copy = pltpu.make_async_copy(source.at[part], target.at[part], arrived.at[k, c])
            copy.start()
            copies.append(copy)
    for c in range(OUT_CHUNKS):
        part = pl.ds(c * wide, wide)
        for k, (source, target) in enumerate(((grad_out, gout), (error_out, eout))):
            copy = pltpu.make_async_copy(
                source.at[:, part], target.at[:, part], arrived.at[2 + k, c]
            )
            copy.start()
            copies.append(copy)
    right = warm_kv[...].astype(bf16)
    even = jnp.full((8, LANES), core[0], jnp.int32) == 0
    for c in range(KV_CHUNKS):
        copies[2 * c].wait()
        copies[2 * c + 1].wait()
        part = pl.ds(c * rows, rows)
        merged = merge(gkv[part, :], ekv[part, :])
        merged_kv[part, :] = merged
        sketch = lax.dot_general(
            right, merged, (((1,), (1,)), ((), ())), preferred_element_type=f32
        )
        for k in range(4):
            zero = sketch[:, k * LANES : (k + 1) * LANES]
            one = sketch[:, (k + 4) * LANES : (k + 5) * LANES]
            keep[c, k] = jnp.where(even, zero, one)
            give[c, k] = jnp.where(even, one, zero)
    total = None
    for c in range(OUT_CHUNKS):
        index = 2 * KV_CHUNKS + 2 * c
        copies[index].wait()
        copies[index + 1].wait()
        part = pl.ds(c * wide, wide)
        merged = merge(gout[:, part], eout[:, part])
        merged_out[:, part] = merged
        sketch = lax.dot_general(
            warm_out[:, part].astype(bf16),
            merged,
            (((1,), (1,)), ((), ())),
            preferred_element_type=f32,
        )
        total = sketch if total is None else total + sketch
    for z in range(8):
        for k in range(2):
            tile = total[:, k * LANES : (k + 1) * LANES]
            keep[z, 4 + k] = tile
            give[z, 4 + k] = tile


def total_of(received, index):
    value = received[0, index]
    for d in range(1, received.shape[0]):
        value = value + received[d, index]
    return value


def second(received, merged_out, send, sketch_out):
    tiles = [total_of(received, k) for k in range(6)]
    sketch_out[0] = tiles[4]
    sketch_out[1] = tiles[5]
    gram = jnp.zeros((8, LANES), f32)
    lane = lax.broadcasted_iota(jnp.int32, (8, LANES), 1)
    for j, column in enumerate(gram_columns(tiles[4:6])):
        gram = jnp.where(lane == j, column, gram)
    high, low = split(jnp.concatenate(tiles[4:6], axis=1))
    left = jnp.concatenate([high.astype(f32), low.astype(f32)], axis=0).astype(bf16)
    for c in range(4):
        both = jnp.dot(left, merged_out[:, c * 1024 : (c + 1) * 1024], preferred_element_type=f32)
        both = both[:8] + both[8:]
        for k in range(8):
            tile = 8 * c + k
            send[tile // 2, 4 + tile % 2] = both[:, k * LANES : (k + 1) * LANES]
    for d in range(16):
        for k in range(4):
            send[d, k] = tiles[k]
        send[d, 6] = gram


def third(received, send, gram):
    tiles = [total_of(received, k) for k in range(7)]
    for z in range(8):
        for k in range(6):
            send[z, k] = tiles[k]
    gram[...] = tiles[6]


def fourth_out(mine, other, send):
    for k in range(2):
        value = total_of(mine, 4 + k) + total_of(other, 4 + k)
        for d in range(16):
            send[d, k] = value


def fourth_kv(core, mine, other, merged_kv, send, basis):
    even = jnp.full((8, LANES), core[0], jnp.int32) == 0
    tiles = []
    for z in range(8):
        for k in range(4):
            tiles.append(jnp.where(even, mine[z, k], other[z, k]))
        for k in range(4):
            tiles.append(jnp.where(even, other[z, k], mine[z, k]))
    steps, scale = cholesky(gram_columns(tiles))
    term = jnp.zeros((8, LANES), f32)
    for c in range(8):
        done = []
        for k in range(8):
            value = substitute(tiles[8 * c + k], steps, scale)
            basis[:, (8 * c + k) * LANES : (8 * c + k + 1) * LANES] = value
            done.append(value)
        low = jnp.concatenate(done, axis=1).astype(bf16)
        term = term + jnp.dot(
            low, merged_kv[c * 1024 : (c + 1) * 1024, :], preferred_element_type=f32
        )
    for d in range(16):
        send[d] = term


def finish_out(received, gram, sketch_out, merged_out, factor, residual, done, sent):
    lane = lax.broadcasted_iota(jnp.int32, (8, LANES), 1)
    columns = [
        jnp.broadcast_to(
            jnp.sum(jnp.where(lane == j, gram[...], 0.0), axis=1, keepdims=True), (8, LANES)
        )
        for j in range(8)
    ]
    steps, scale = cholesky(columns)
    basis = [substitute(sketch_out[k], steps, scale) for k in range(2)]
    left = left_terms(jnp.concatenate(basis, axis=1))
    copies = []
    wide = 1024
    for c in range(4):
        values = []
        for k in range(8):
            tile = 8 * c + k
            value = substitute(received[tile // 2, tile % 2], steps, scale) * (1.0 / 16.0)
            factor[:, tile * LANES : (tile + 1) * LANES] = value
            values.append(value)
        right = right_terms(jnp.concatenate(values, axis=1))
        part = pl.ds(c * wide, wide)
        approx = jnp.dot(left, right, preferred_element_type=f32)
        done[:, part] = (merged_out[:, part].astype(f32) - approx).astype(bf16)
        copy = pltpu.make_async_copy(done.at[:, part], residual.at[:, part], sent.at[c])
        copy.start()
        copies.append(copy)
    for copy in copies:
        copy.wait()


def finish_kv(received, basis, merged_kv, factor, residual, done, sent):
    value = received[0]
    for d in range(1, 16):
        value = value + received[d]
    value = value * (1.0 / 16.0)
    factor[...] = value
    right = right_terms(value)
    copies = []
    rows = 1024
    for c in range(8):
        part = pl.ds(c * rows, rows)
        left = left_terms(basis[:, part])
        approx = jnp.dot(left, right, preferred_element_type=f32)
        done[part, :] = (merged_kv[part, :].astype(f32) - approx).astype(bf16)
        copy = pltpu.make_async_copy(done.at[part], residual.at[part], sent.at[c])
        copy.start()
        copies.append(copy)
    for copy in copies:
        copy.wait()


def exchange(value, axis, groups=None):
    return lax.all_to_all(value, axis, 0, 0, axis_index_groups=groups)


def per_device(grad_kv, error_kv, grad_out, error_out, warm_kv, warm_out):
    grad_kv, error_kv, grad_out, error_out = (
        value[0] for value in (grad_kv, error_kv, grad_out, error_out)
    )
    kv_shape, out_shape = grad_kv.shape, grad_out.shape
    far = pl.BlockSpec(memory_space=pltpu.HBM)
    scalar = pl.BlockSpec(memory_space=pltpu.SMEM)
    columns = [[2 * z + c for z in range(8)] for c in range(2)]
    swap = [(d, d ^ 1) for d in range(16)]
    core = (lax.axis_index("dp") % 2).astype(jnp.int32).reshape(1)
    merged_kv, merged_out, keep, give = pl.pallas_call(
        first,
        out_shape=(
            pltpu.VMEM(kv_shape, bf16),
            pltpu.VMEM(out_shape, bf16),
            pltpu.VMEM((8, 6, 8, LANES), f32),
            pltpu.VMEM((8, 6, 8, LANES), f32),
        ),
        in_specs=[scalar] + [far] * 4 + [whole] * 2,
        out_specs=(whole,) * 4,
        scratch_shapes=[
            pltpu.VMEM(kv_shape, bf16),
            pltpu.VMEM(kv_shape, bf16),
            pltpu.VMEM(out_shape, bf16),
            pltpu.VMEM(out_shape, bf16),
            pltpu.SemaphoreType.DMA((4, 8)),
        ],
        compiler_params=limit,
        name="first",
    )(core, *(distant(v) for v in (grad_kv, error_kv, grad_out, error_out)), warm_kv.T, warm_out.T)

    received = exchange(keep + lax.ppermute(give, "dp", swap), "dp", columns)
    send, sketch_out = pl.pallas_call(
        second,
        out_shape=(pltpu.VMEM((16, 7, 8, LANES), f32), pltpu.VMEM((2, 8, LANES), f32)),
        in_specs=[whole] * 2,
        out_specs=(whole,) * 2,
        compiler_params=limit,
        name="second",
    )(resident(received), resident(merged_out))

    received = exchange(send, "tensor")
    send, gram = pl.pallas_call(
        third,
        out_shape=(pltpu.VMEM((8, 6, 8, LANES), f32), pltpu.VMEM((8, LANES), f32)),
        in_specs=[whole],
        out_specs=(whole,) * 2,
        compiler_params=limit,
        name="third",
    )(resident(received))

    mine = exchange(send, "dp", columns)
    other = lax.ppermute(mine, "dp", swap)
    send_out = pl.pallas_call(
        fourth_out,
        out_shape=pltpu.VMEM((16, 2, 8, LANES), f32),
        in_specs=[whole] * 2,
        out_specs=whole,
        compiler_params=limit,
        name="fourth_out",
    )(resident(mine), resident(other))
    received_out = exchange(send_out, "tensor")

    send_kv, basis = pl.pallas_call(
        fourth_kv,
        out_shape=(pltpu.VMEM((16, 8, LANES), f32), pltpu.VMEM((8, kv_shape[0]), f32)),
        in_specs=[scalar] + [whole] * 3,
        out_specs=(whole,) * 2,
        compiler_params=limit,
        name="fourth_kv",
    )(core, resident(mine), resident(other), resident(merged_kv))
    received_kv = exchange(send_kv, "dp")

    factor_out, residual_out = pl.pallas_call(
        finish_out,
        out_shape=(
            jax.ShapeDtypeStruct((8, out_shape[1]), f32),
            pltpu.HBM(out_shape, bf16),
        ),
        in_specs=[whole] * 4,
        out_specs=(whole, far),
        scratch_shapes=[pltpu.VMEM(out_shape, bf16), pltpu.SemaphoreType.DMA((4,))],
        compiler_params=limit,
        name="finish_out",
    )(resident(received_out), resident(gram), resident(sketch_out), resident(merged_out))

    factor_kv, residual_kv = pl.pallas_call(
        finish_kv,
        out_shape=(
            jax.ShapeDtypeStruct((8, kv_shape[1]), f32),
            pltpu.HBM(kv_shape, bf16),
        ),
        in_specs=[whole] * 3,
        out_specs=(whole, far),
        scratch_shapes=[pltpu.VMEM(kv_shape, bf16), pltpu.SemaphoreType.DMA((8,))],
        compiler_params=limit,
        name="finish_kv",
    )(resident(received_kv), resident(basis), resident(merged_kv))

    return factor_kv.T, factor_out.T, residual_kv[None], residual_out[None]


def solution(mesh):
    placed = (
        P("dp", None, "tensor"),
        P("dp", None, "tensor"),
        P("dp", "tensor", None),
        P("dp", "tensor", None),
        P("tensor", None),
        P(),
    )
    return jax.shard_map(
        per_device,
        mesh=mesh,
        in_specs=placed,
        out_specs=(P("tensor", None), P(), P("dp", None, "tensor"), P("dp", "tensor", None)),
        check_vma=False,
    )
```

```python
import jax
import jax.numpy as jnp
from jax import lax
from jax.experimental import pallas as pl
from jax.experimental.pallas import tpu as pltpu
from jax.sharding import PartitionSpec as P

epsilon = 1e-06
f32 = jnp.float32
bf16 = jnp.bfloat16
LANES = 128
KV_CHUNKS = 4
OUT_CHUNKS = 4
limit = pltpu.CompilerParams(vmem_limit_bytes=24 * 1024 * 1024)
whole = pl.BlockSpec(memory_space=pltpu.VMEM)


def resident(value):
    return pltpu.with_memory_space_constraint(value, pltpu.VMEM)


def distant(value):
    return pltpu.with_memory_space_constraint(value, pltpu.HBM)


def merge(grad, error):
    return (grad.astype(f32) + error.astype(f32)).astype(bf16)


def split(value):
    high = value.astype(bf16)
    low = (value - high.astype(f32)).astype(bf16)
    return high, low


def row(tile, index):
    return jnp.broadcast_to(tile[index : index + 1, :], tile.shape)


def gram_columns(tiles):
    sums = [None] * 8
    for tile in tiles:
        for j in range(8):
            product = tile * row(tile, j)
            sums[j] = product if sums[j] is None else sums[j] + product
    return [
        jnp.broadcast_to(jnp.sum(total, axis=1, keepdims=True), (8, LANES)) for total in sums
    ]


def cholesky(columns):
    place = lax.broadcasted_iota(jnp.int32, (8, LANES), 0)
    columns = [
        column + jnp.where(place == j, epsilon, 0.0).astype(f32)
        for j, column in enumerate(columns)
    ]
    steps = []
    scale = jnp.zeros((8, LANES), f32)
    for j in range(8):
        inverse = lax.rsqrt(jnp.maximum(row(columns[j], j), epsilon))
        lower = jnp.where(place > j, columns[j] * inverse, 0.0)
        for k in range(j + 1, 8):
            columns[k] = columns[k] - lower * row(lower, k)
        steps.append(lower * inverse)
        scale = jnp.where(place == j, inverse, scale)
    return steps, scale


def substitute(tile, steps, scale):
    for j in range(7):
        tile = tile - steps[j] * row(tile, j)
    return tile * scale


def left_terms(value):
    high, low = split(value)
    high, low = high.astype(f32), low.astype(f32)
    return jnp.concatenate([high, low, high, jnp.zeros_like(high)], axis=0).T.astype(bf16)


def right_terms(value):
    high, low = split(value)
    high, low = high.astype(f32), low.astype(f32)
    return jnp.concatenate([high, high, low, jnp.zeros_like(high)], axis=0).astype(bf16)


def block(index, size):
    start = index * size
    return pl.ds(start if isinstance(index, int) else pl.multiple_of(start, size), size)


def first_out(grad, error, warm, merged_out, send, warm_near, near, far_, arrived, warm_arrived):
    wide = near.shape[1] // OUT_CHUNKS

    def copies(c):
        part = block(c, wide)
        return [
            pltpu.make_async_copy(source.at[:, part], target.at[:, part], arrived.at[k, c])
            for k, (source, target) in enumerate(((grad, near), (error, far_)))
        ]

    warm_copy = pltpu.make_async_copy(warm, warm_near, warm_arrived)
    warm_copy.start()

    @pl.loop(0, OUT_CHUNKS)
    def _(c):
        for copy in copies(c):
            copy.start()

    warm_copy.wait()

    def step(c, total):
        for copy in copies(c):
            copy.wait()
        part = block(c, wide)
        merged = merge(near[:, part], far_[:, part])
        merged_out[:, part] = merged
        return total + lax.dot_general(
            warm_near[:, part].astype(bf16),
            merged,
            (((1,), (1,)), ((), ())),
            preferred_element_type=f32,
        )

    total = lax.fori_loop(0, OUT_CHUNKS, step, jnp.zeros((8, near.shape[0]), f32))
    for d in range(16):
        for k in range(2):
            send[d, k] = total[:, k * LANES : (k + 1) * LANES]


def first_kv(core, grad, error, warm, merged_out, merged_kv, stored_out, keep, give, warm_near,
             near, far_, done, arrived, sent, warm_arrived, out_sent):
    rows = near.shape[0] // KV_CHUNKS

    def copies(c):
        part = block(c, rows)
        return [
            pltpu.make_async_copy(source.at[part], target.at[part], arrived.at[k, c])
            for k, (source, target) in enumerate(((grad, near), (error, far_)))
        ]

    def leaving(c):
        part = block(c, rows)
        return pltpu.make_async_copy(done.at[part], merged_kv.at[part], sent.at[c])

    warm_copy = pltpu.make_async_copy(warm, warm_near, warm_arrived)
    warm_copy.start()

    @pl.loop(0, KV_CHUNKS)
    def _(c):
        for copy in copies(c):
            copy.start()

    warm_copy.wait()
    out_copy = pltpu.make_async_copy(merged_out, stored_out, out_sent)
    out_copy.start()
    right = warm_near[...].astype(bf16)
    even = jnp.full((8, LANES), core[0], jnp.int32) == 0
    for c in range(KV_CHUNKS):
        for copy in copies(c):
            copy.wait()
        part = block(c, rows)
        merged = merge(near[part, :], far_[part, :])
        done[part, :] = merged
        leaving(c).start()
        sketch = lax.dot_general(
            right, merged, (((1,), (1,)), ((), ())), preferred_element_type=f32
        )
        for t in range(4):
            for k in range(2):
                first = (4 * t + k) * LANES
                zero = sketch[:, first : first + LANES]
                one = sketch[:, first + 2 * LANES : first + 3 * LANES]
                keep[4 * c + t, k] = jnp.where(even, zero, one)
                give[4 * c + t, k] = jnp.where(even, one, zero)

    out_copy.wait()

    @pl.loop(0, KV_CHUNKS)
    def _(c):
        leaving(c).wait()


def total_of(received, index):
    value = received[0, index]
    for d in range(1, received.shape[0]):
        value = value + received[d, index]
    return value


def second(core, received, merged_out, merged_kv, keep, give, sketch_out, same_kv):
    del merged_kv, same_kv
    tiles = [total_of(received, k) for k in range(2)]
    sketch_out[0] = tiles[0]
    sketch_out[1] = tiles[1]
    even = jnp.full((8, LANES), core[0], jnp.int32) == 0
    value = jnp.concatenate(tiles, axis=1)
    high = value.astype(bf16)
    middle, low = split(value - high.astype(f32))
    left = jnp.concatenate(
        [part.astype(f32) for part in (high, middle, low, jnp.zeros_like(low))], axis=0
    ).astype(bf16)
    for c in range(4):
        terms = jnp.dot(left, merged_out[:, c * 1024 : (c + 1) * 1024], preferred_element_type=f32)
        total = terms[:8] + (terms[8:16] + terms[16:24])
        for t in range(4):
            first = 2 * t * LANES
            zero = total[:, first : first + LANES]
            one = total[:, first + LANES : first + 2 * LANES]
            keep[4 * c + t, 0] = jnp.where(even, zero, one)
            give[4 * c + t, 0] = jnp.where(even, one, zero)


def third(received, send):
    tiles = [total_of(received, k) for k in range(3)]
    for z in range(8):
        for k in range(3):
            send[z, k] = tiles[k]


def fourth(received, send):
    tiles = [total_of(received, k) for k in range(3)]
    for t in range(16):
        for k in range(3):
            send[t, k] = tiles[k]


def in_order(core, mine, other, first, count):
    even = jnp.full((8, LANES), core[0], jnp.int32) == 0
    tiles = []
    for t in range(16):
        for k in range(first, first + count):
            tiles.append(jnp.where(even, mine[t, k], other[t, k]))
        for k in range(first, first + count):
            tiles.append(jnp.where(even, other[t, k], mine[t, k]))
    return tiles


def partial_factor(core, which, tiles, merged_kv):
    base = lax.rem(core[0] + which, 2) * 256
    term = jnp.zeros((16, LANES), f32)
    for t in range(16):
        high, low = split(jnp.concatenate([tiles[t, 0], tiles[t, 1]], axis=1))
        left = jnp.concatenate([high.astype(f32), low.astype(f32)], axis=0).astype(bf16)
        rows = pl.ds(pl.multiple_of(t * 512 + base, 256), 256)
        term = term + jnp.dot(left, merged_kv[rows, :], preferred_element_type=f32)
    return term[:8] + term[8:]


def fifth_mine(core, mine, merged_kv, term):
    term[...] = partial_factor(core, 0, mine, merged_kv)


def fifth_other(core, other, merged_kv, begun, send):
    term = begun[...] + partial_factor(core, 1, other, merged_kv)
    for d in range(16):
        send[d] = term


def orthonormal_kv(core, mine, other, basis, lower, scale):
    tiles = in_order(core, mine, other, 0, 2)
    steps, inverse = cholesky(gram_columns(tiles))
    for j in range(8):
        lower[j] = steps[j]
    scale[...] = inverse
    for k, tile in enumerate(tiles):
        basis[:, k * LANES : (k + 1) * LANES] = substitute(tile, steps, inverse)


def finish_out(core, mine, other, warm, sketch_out, merged_out, factor, residual, near, done,
               factor_near, warm_near, arrived, sent, factor_sent, warm_arrived):
    wide = done.shape[1] // 4

    def arriving(c):
        part = block(c, wide)
        return pltpu.make_async_copy(merged_out.at[:, part], near.at[:, part], arrived.at[c])

    def leaving(c):
        part = block(c, wide)
        return pltpu.make_async_copy(done.at[:, part], residual.at[:, part], sent.at[c])

    warm_copy = pltpu.make_async_copy(warm, warm_near, warm_arrived)
    warm_copy.start()

    @pl.loop(0, 4)
    def _(c):
        arriving(c).start()

    values = in_order(core, mine, other, 2, 1)
    warm_copy.wait()
    sums = [jnp.zeros((8, LANES), f32)] * 8
    for k, tile in enumerate(values):
        right = warm_near[:, k * LANES : (k + 1) * LANES].astype(bf16).astype(f32)
        for j in range(8):
            sums[j] = sums[j] + right * row(tile, j)
    steps, scale = cholesky(
        [jnp.broadcast_to(jnp.sum(total, axis=1, keepdims=True), (8, LANES)) for total in sums]
    )
    basis = [substitute(sketch_out[k], steps, scale) for k in range(2)]
    left = left_terms(jnp.concatenate(basis, axis=1))
    values = [substitute(tile, steps, scale) * (1.0 / 16.0) for tile in values]
    for k, value in enumerate(values):
        factor_near[:, k * LANES : (k + 1) * LANES] = value
    factor_copy = pltpu.make_async_copy(factor_near, factor, factor_sent)
    factor_copy.start()
    for c in range(4):
        right = right_terms(jnp.concatenate(values[8 * c : 8 * c + 8], axis=1))
        part = block(c, wide)
        approx = jnp.dot(left, right, preferred_element_type=f32)
        arriving(c).wait()
        done[:, part] = (near[:, part].astype(f32) - approx).astype(bf16)
        leaving(c).start()

    @pl.loop(0, 4)
    def _(c):
        leaving(c).wait()

    factor_copy.wait()


def finish_kv(received, lower, scale, basis, merged_kv, factor, residual, done, factor_near, sent,
              factor_sent):
    rows = 1024

    def leaving(c):
        part = block(c, rows)
        return pltpu.make_async_copy(done.at[part], residual.at[part], sent.at[c])

    value = received[0]
    for d in range(1, 16):
        value = value + received[d]
    value = substitute(value, [lower[j] for j in range(8)], scale[...]) * (1.0 / 16.0)
    factor_near[...] = value
    factor_copy = pltpu.make_async_copy(factor_near, factor, factor_sent)
    factor_copy.start()
    right = right_terms(value)
    for c in range(8):
        part = block(c, rows)
        left = left_terms(basis[:, part])
        approx = jnp.dot(left, right, preferred_element_type=f32)
        done[part, :] = (merged_kv[part, :].astype(f32) - approx).astype(bf16)
        leaving(c).start()

    @pl.loop(0, 8)
    def _(c):
        leaving(c).wait()

    factor_copy.wait()


def exchange(value, axis, groups=None):
    return lax.all_to_all(value, axis, 0, 0, axis_index_groups=groups)


def call(kernel, outs, ins, args, scratch=(), seconds=1.0, aliases=None):
    return pl.pallas_call(
        kernel,
        out_shape=outs,
        in_specs=ins,
        out_specs=jax.tree.map(
            lambda out: far if isinstance(out, pl.MemoryRef) and out.memory_space == pltpu.HBM else whole,
            outs,
            is_leaf=lambda out: not isinstance(out, tuple),
        ),
        scratch_shapes=list(scratch),
        input_output_aliases=aliases or {},
        compiler_params=limit,
        cost_estimate=pl.CostEstimate(
            flops=0, bytes_accessed=int(seconds * 2_000_000), transcendentals=0
        ),
        name=kernel.__name__,
    )(*args)


far = pl.BlockSpec(memory_space=pltpu.HBM)
scalar = pl.BlockSpec(memory_space=pltpu.SMEM)


def per_device(grad_kv, error_kv, grad_out, error_out, warm_kv, warm_out):
    grad_kv, error_kv, grad_out, error_out = (
        distant(value[0]) for value in (grad_kv, error_kv, grad_out, error_out)
    )
    kv_shape, out_shape = grad_kv.shape, grad_out.shape
    columns = [[2 * z + c for z in range(8)] for c in range(2)]
    swap = [(d, d ^ 1) for d in range(16)]
    core = (lax.axis_index("dp") % 2).astype(jnp.int32).reshape(1)

    def tiles(*lead):
        return pltpu.VMEM((*lead, 8, LANES), f32)

    merged_out, send = call(
        first_out,
        (pltpu.VMEM(out_shape, bf16), tiles(16, 2)),
        [far] * 3,
        (grad_out, error_out, distant(warm_out.T)),
        [
            pltpu.VMEM((8, out_shape[1]), f32),
            pltpu.VMEM(out_shape, bf16),
            pltpu.VMEM(out_shape, bf16),
            pltpu.SemaphoreType.DMA((2, OUT_CHUNKS)),
            pltpu.SemaphoreType.DMA,
        ],
        2.6,
    )
    received = exchange(send, "dp")
    merged_kv, stored, keep_kv, give_kv = call(
        first_kv,
        (pltpu.HBM(kv_shape, bf16), pltpu.HBM(out_shape, bf16), tiles(16, 2), tiles(16, 2)),
        [scalar] + [far] * 3 + [whole],
        (core, grad_kv, error_kv, distant(warm_kv.T), resident(merged_out)),
        [
            pltpu.VMEM((8, kv_shape[1]), f32),
            pltpu.VMEM(kv_shape, bf16),
            pltpu.VMEM(kv_shape, bf16),
            pltpu.VMEM(kv_shape, bf16),
            pltpu.SemaphoreType.DMA((2, KV_CHUNKS)),
            pltpu.SemaphoreType.DMA((KV_CHUNKS,)),
            pltpu.SemaphoreType.DMA,
            pltpu.SemaphoreType.DMA,
        ],
        2.6,
    )
    keep_out, give_out, sketch_out, merged_kv = call(
        second,
        (tiles(16, 1), tiles(16, 1), tiles(2), pltpu.HBM(kv_shape, bf16)),
        [scalar] + [whole] * 2 + [far],
        (core, resident(received), resident(merged_out), distant(merged_kv)),
        seconds=0.4,
        aliases={3: 3},
    )
    kv = keep_kv + lax.ppermute(give_kv, "dp", swap)
    out = keep_out + lax.ppermute(give_out, "dp", swap)
    received = exchange(jnp.concatenate([kv, out], axis=1), "tensor")
    send = call(third, tiles(8, 3), [whole], (resident(received),), seconds=0.1)
    received = exchange(send, "dp", columns)
    send = call(fourth, tiles(16, 3), [whole], (resident(received),), seconds=0.1)
    mine = exchange(send, "tensor")
    other = lax.ppermute(mine, "dp", swap)
    begun = call(
        fifth_mine,
        tiles(),
        [scalar] + [whole] * 2,
        (core, resident(mine), resident(merged_kv)),
        seconds=0.5,
    )
    send = call(
        fifth_other,
        tiles(16),
        [scalar] + [whole] * 3,
        (core, resident(other), resident(merged_kv), resident(begun)),
        seconds=0.5,
    )
    received = exchange(send, "dp")
    basis, lower, scale = call(
        orthonormal_kv,
        (pltpu.VMEM((8, kv_shape[0]), f32), tiles(8), tiles()),
        [scalar] + [whole] * 2,
        (core, resident(mine), resident(other)),
    )
    factor_out, residual_out = call(
        finish_out,
        (pltpu.HBM((8, out_shape[1]), f32), pltpu.HBM(out_shape, bf16)),
        [scalar] + [whole] * 2 + [far, whole, far],
        (
            core,
            resident(mine),
            resident(other),
            distant(warm_out.T),
            resident(sketch_out),
            distant(stored),
        ),
        [
            pltpu.VMEM(out_shape, bf16),
            pltpu.VMEM(out_shape, bf16),
            pltpu.VMEM((8, out_shape[1]), f32),
            pltpu.VMEM((8, out_shape[1]), f32),
            pltpu.SemaphoreType.DMA((4,)),
            pltpu.SemaphoreType.DMA((4,)),
            pltpu.SemaphoreType.DMA,
            pltpu.SemaphoreType.DMA,
        ],
        2.5,
    )
    factor_kv, residual_kv = call(
        finish_kv,
        (pltpu.HBM((8, kv_shape[1]), f32), pltpu.HBM(kv_shape, bf16)),
        [whole] * 5,
        tuple(resident(value) for value in (received, lower, scale, basis, merged_kv)),
        [
            pltpu.VMEM(kv_shape, bf16),
            pltpu.VMEM((8, kv_shape[1]), f32),
            pltpu.SemaphoreType.DMA((8,)),
            pltpu.SemaphoreType.DMA,
        ],
        2.5,
    )
    return factor_kv.T, factor_out.T, residual_kv[None], residual_out[None]


def solution(mesh):
    placed = (
        P("dp", None, "tensor"),
        P("dp", None, "tensor"),
        P("dp", "tensor", None),
        P("dp", "tensor", None),
        P("tensor", None),
        P(),
    )
    return jax.shard_map(
        per_device,
        mesh=mesh,
        in_specs=placed,
        out_specs=(P("tensor", None), P(), P("dp", None, "tensor"), P("dp", "tensor", None)),
        check_vma=False,
    )
```

```python
import jax
import jax.numpy as jnp
from jax import lax
from jax.experimental import pallas as pl
from jax.experimental.pallas import tpu as pltpu
from jax.sharding import PartitionSpec as P

epsilon = 1e-06
f32 = jnp.float32
bf16 = jnp.bfloat16
LANES = 128
KV_CHUNKS = 4
OUT_CHUNKS = 4
limit = pltpu.CompilerParams(vmem_limit_bytes=24 * 1024 * 1024)
whole = pl.BlockSpec(memory_space=pltpu.VMEM)


def resident(value):
    return pltpu.with_memory_space_constraint(value, pltpu.VMEM)


def distant(value):
    return pltpu.with_memory_space_constraint(value, pltpu.HBM)


def merge(grad, error):
    return (grad.astype(f32) + error.astype(f32)).astype(bf16)


def split(value):
    high = value.astype(bf16)
    low = (value - high.astype(f32)).astype(bf16)
    return high, low


def row(tile, index):
    return jnp.broadcast_to(tile[index : index + 1, :], tile.shape)


def gram_columns(tiles):
    sums = [None] * 8
    for tile in tiles:
        for j in range(8):
            product = tile * row(tile, j)
            sums[j] = product if sums[j] is None else sums[j] + product
    return [
        jnp.broadcast_to(jnp.sum(total, axis=1, keepdims=True), (8, LANES)) for total in sums
    ]


def cholesky(columns):
    place = lax.broadcasted_iota(jnp.int32, (8, LANES), 0)
    columns = [
        column + jnp.where(place == j, epsilon, 0.0).astype(f32)
        for j, column in enumerate(columns)
    ]
    steps = []
    scale = jnp.zeros((8, LANES), f32)
    for j in range(8):
        inverse = lax.rsqrt(jnp.maximum(row(columns[j], j), epsilon))
        lower = jnp.where(place > j, columns[j] * inverse, 0.0)
        for k in range(j + 1, 8):
            columns[k] = columns[k] - lower * row(lower, k)
        steps.append(lower * inverse)
        scale = jnp.where(place == j, inverse, scale)
    return steps, scale


def substitute(tile, steps, scale):
    for j in range(7):
        tile = tile - steps[j] * row(tile, j)
    return tile * scale


def left_terms(value):
    high, low = split(value)
    high, low = high.astype(f32), low.astype(f32)
    return jnp.concatenate([high, low, high, jnp.zeros_like(high)], axis=0).T.astype(bf16)


def right_terms(value):
    high, low = split(value)
    high, low = high.astype(f32), low.astype(f32)
    return jnp.concatenate([high, high, low, jnp.zeros_like(high)], axis=0).astype(bf16)


def block(index, size):
    start = index * size
    return pl.ds(start if isinstance(index, int) else pl.multiple_of(start, size), size)


def first_out(grad, error, warm, merged_out, send, warm_near, near, far_, arrived, warm_arrived):
    wide = near.shape[1] // OUT_CHUNKS

    def copies(c):
        part = block(c, wide)
        return [
            pltpu.make_async_copy(source.at[:, part], target.at[:, part], arrived.at[k, c])
            for k, (source, target) in enumerate(((grad, near), (error, far_)))
        ]

    warm_copy = pltpu.make_async_copy(warm, warm_near, warm_arrived)
    warm_copy.start()

    @pl.loop(0, OUT_CHUNKS)
    def _(c):
        for copy in copies(c):
            copy.start()

    warm_copy.wait()

    def step(c, total):
        for copy in copies(c):
            copy.wait()
        part = block(c, wide)
        merged = merge(near[:, part], far_[:, part])
        merged_out[:, part] = merged
        return total + lax.dot_general(
            warm_near[:, part].astype(bf16),
            merged,
            (((1,), (1,)), ((), ())),
            preferred_element_type=f32,
        )

    total = lax.fori_loop(0, OUT_CHUNKS, step, jnp.zeros((8, near.shape[0]), f32))
    for d in range(16):
        for k in range(2):
            send[d, k] = total[:, k * LANES : (k + 1) * LANES]


def first_kv(core, grad, error, warm, merged_out, merged_kv, stored_out, keep, give, warm_near,
             near, far_, done, arrived, sent, warm_arrived, out_sent):
    rows = near.shape[0] // KV_CHUNKS

    def copies(c):
        part = block(c, rows)
        return [
            pltpu.make_async_copy(source.at[part], target.at[part], arrived.at[k, c])
            for k, (source, target) in enumerate(((grad, near), (error, far_)))
        ]

    def leaving(c):
        part = block(c, rows)
        return pltpu.make_async_copy(done.at[part], merged_kv.at[part], sent.at[c])

    warm_copy = pltpu.make_async_copy(warm, warm_near, warm_arrived)
    warm_copy.start()

    @pl.loop(0, KV_CHUNKS)
    def _(c):
        for copy in copies(c):
            copy.start()

    warm_copy.wait()
    out_copy = pltpu.make_async_copy(merged_out, stored_out, out_sent)
    out_copy.start()
    right = warm_near[...].astype(bf16)
    even = jnp.full((8, LANES), core[0], jnp.int32) == 0
    for c in range(KV_CHUNKS):
        for copy in copies(c):
            copy.wait()
        part = block(c, rows)
        merged = merge(near[part, :], far_[part, :])
        done[part, :] = merged
        leaving(c).start()
        sketch = lax.dot_general(
            right, merged, (((1,), (1,)), ((), ())), preferred_element_type=f32
        )
        for t in range(4):
            for k in range(2):
                first = (4 * t + k) * LANES
                zero = sketch[:, first : first + LANES]
                one = sketch[:, first + 2 * LANES : first + 3 * LANES]
                keep[4 * c + t, k] = jnp.where(even, zero, one)
                give[4 * c + t, k] = jnp.where(even, one, zero)

    out_copy.wait()

    @pl.loop(0, KV_CHUNKS)
    def _(c):
        leaving(c).wait()


def total_of(received, index):
    value = received[0, index]
    for d in range(1, received.shape[0]):
        value = value + received[d, index]
    return value


def half_factor(left, merged_out, half, target):
    wide = merged_out.shape[1] // 4
    for c in range(2):
        part = pl.ds(pl.multiple_of((2 * half + c) * wide, wide), wide)
        terms = jnp.dot(left, merged_out[:, part], preferred_element_type=f32)
        total = terms[:8] + (terms[8:16] + terms[16:24])
        for t in range(8):
            target[8 * c + t, 0] = total[:, t * LANES : (t + 1) * LANES]


def second_give(core, received, merged_out, give, sketch_out, terms):
    tiles = [total_of(received, k) for k in range(2)]
    sketch_out[0] = tiles[0]
    sketch_out[1] = tiles[1]
    value = jnp.concatenate(tiles, axis=1)
    high = value.astype(bf16)
    middle, low = split(value - high.astype(f32))
    left = jnp.concatenate(
        [part.astype(f32) for part in (high, middle, low, jnp.zeros_like(low))], axis=0
    ).astype(bf16)
    terms[...] = left
    half_factor(left, merged_out, 1 - core[0], give)


def second_keep(core, terms, merged_out, merged_kv, keep, same_kv):
    del merged_kv, same_kv
    half_factor(terms[...], merged_out, core[0], keep)


def third(received, send):
    tiles = [total_of(received, k) for k in range(3)]
    for z in range(8):
        for k in range(3):
            send[z, k] = tiles[k]


def fourth(received, send):
    tiles = [total_of(received, k) for k in range(3)]
    for t in range(16):
        for k in range(3):
            send[t, k] = tiles[k]


def in_order(core, mine, other):
    even = jnp.full((8, LANES), core[0], jnp.int32) == 0
    tiles = []
    for t in range(16):
        for k in range(2):
            tiles.append(jnp.where(even, mine[t, k], other[t, k]))
        for k in range(2):
            tiles.append(jnp.where(even, other[t, k], mine[t, k]))
    return tiles


def partial_factor(core, which, tiles, merged_kv):
    base = lax.rem(core[0] + which, 2) * 256
    term = jnp.zeros((16, LANES), f32)
    for t in range(16):
        high, low = split(jnp.concatenate([tiles[t, 0], tiles[t, 1]], axis=1))
        left = jnp.concatenate([high.astype(f32), low.astype(f32)], axis=0).astype(bf16)
        rows = pl.ds(pl.multiple_of(t * 512 + base, 256), 256)
        term = term + jnp.dot(left, merged_kv[rows, :], preferred_element_type=f32)
    return term[:8] + term[8:]


def fifth_mine(core, mine, merged_kv, term):
    term[...] = partial_factor(core, 0, mine, merged_kv)


def fifth_other(core, other, merged_kv, begun, send):
    term = begun[...] + partial_factor(core, 1, other, merged_kv)
    for d in range(16):
        send[d] = term


def orthonormal_kv(core, mine, other, basis, lower, scale):
    tiles = in_order(core, mine, other)
    steps, inverse = cholesky(gram_columns(tiles))
    for j in range(8):
        lower[j] = steps[j]
    scale[...] = inverse
    for k, tile in enumerate(tiles):
        basis[:, k * LANES : (k + 1) * LANES] = substitute(tile, steps, inverse)


def finish_out(core, mine, other, warm, sketch_out, merged_out, factor, residual, near, done,
               factor_near, warm_near, arrived, sent, factor_sent, warm_arrived):
    wide = done.shape[1] // 4

    def arriving(c):
        part = block(c, wide)
        return pltpu.make_async_copy(merged_out.at[:, part], near.at[:, part], arrived.at[c])

    def leaving(c):
        part = block(c, wide)
        return pltpu.make_async_copy(done.at[:, part], residual.at[:, part], sent.at[c])

    warm_copy = pltpu.make_async_copy(warm, warm_near, warm_arrived)
    warm_copy.start()

    @pl.loop(0, 4)
    def _(c):
        arriving(c).start()

    even = jnp.full((8, LANES), core[0], jnp.int32) == 0
    values = [jnp.where(even, mine[t, 2], other[t, 2]) for t in range(16)]
    values += [jnp.where(even, other[t, 2], mine[t, 2]) for t in range(16)]
    warm_copy.wait()
    sums = [jnp.zeros((8, LANES), f32)] * 8
    for k, tile in enumerate(values):
        right = warm_near[:, k * LANES : (k + 1) * LANES].astype(bf16).astype(f32)
        for j in range(8):
            sums[j] = sums[j] + right * row(tile, j)
    steps, scale = cholesky(
        [jnp.broadcast_to(jnp.sum(total, axis=1, keepdims=True), (8, LANES)) for total in sums]
    )
    basis = [substitute(sketch_out[k], steps, scale) for k in range(2)]
    left = left_terms(jnp.concatenate(basis, axis=1))
    values = [substitute(tile, steps, scale) * (1.0 / 16.0) for tile in values]
    for k, value in enumerate(values):
        factor_near[:, k * LANES : (k + 1) * LANES] = value
    factor_copy = pltpu.make_async_copy(factor_near, factor, factor_sent)
    factor_copy.start()
    for c in range(4):
        right = right_terms(jnp.concatenate(values[8 * c : 8 * c + 8], axis=1))
        part = block(c, wide)
        approx = jnp.dot(left, right, preferred_element_type=f32)
        arriving(c).wait()
        done[:, part] = (near[:, part].astype(f32) - approx).astype(bf16)
        leaving(c).start()

    @pl.loop(0, 4)
    def _(c):
        leaving(c).wait()

    factor_copy.wait()


def finish_kv(received, lower, scale, basis, merged_kv, factor, residual, done, factor_near, sent,
              factor_sent):
    rows = 1024

    def leaving(c):
        part = block(c, rows)
        return pltpu.make_async_copy(done.at[part], residual.at[part], sent.at[c])

    value = received[0]
    for d in range(1, 16):
        value = value + received[d]
    value = substitute(value, [lower[j] for j in range(8)], scale[...]) * (1.0 / 16.0)
    factor_near[...] = value
    factor_copy = pltpu.make_async_copy(factor_near, factor, factor_sent)
    factor_copy.start()
    right = right_terms(value)
    for c in range(8):
        part = block(c, rows)
        left = left_terms(basis[:, part])
        approx = jnp.dot(left, right, preferred_element_type=f32)
        done[part, :] = (merged_kv[part, :].astype(f32) - approx).astype(bf16)
        leaving(c).start()

    @pl.loop(0, 8)
    def _(c):
        leaving(c).wait()

    factor_copy.wait()


def exchange(value, axis, groups=None):
    return lax.all_to_all(value, axis, 0, 0, axis_index_groups=groups)


def call(kernel, outs, ins, args, scratch=(), seconds=1.0, aliases=None):
    return pl.pallas_call(
        kernel,
        out_shape=outs,
        in_specs=ins,
        out_specs=jax.tree.map(
            lambda out: far if isinstance(out, pl.MemoryRef) and out.memory_space == pltpu.HBM else whole,
            outs,
            is_leaf=lambda out: not isinstance(out, tuple),
        ),
        scratch_shapes=list(scratch),
        input_output_aliases=aliases or {},
        compiler_params=limit,
        cost_estimate=pl.CostEstimate(
            flops=0, bytes_accessed=int(seconds * 2_000_000), transcendentals=0
        ),
        name=kernel.__name__,
    )(*args)


far = pl.BlockSpec(memory_space=pltpu.HBM)
scalar = pl.BlockSpec(memory_space=pltpu.SMEM)


def per_device(grad_kv, error_kv, grad_out, error_out, warm_kv, warm_out):
    grad_kv, error_kv, grad_out, error_out = (
        distant(value[0]) for value in (grad_kv, error_kv, grad_out, error_out)
    )
    kv_shape, out_shape = grad_kv.shape, grad_out.shape
    columns = [[2 * z for z in range(8)], [2 * z + 1 for z in reversed(range(8))]]
    replicas = [[2 * z for z in range(8)] + [2 * z + 1 for z in range(8)]]
    swap = [(d, d ^ 1) for d in range(16)]
    other_way = [15 - t for t in range(16)]
    planes = [
        [(2 * z + c) * 16 + (t if c == 0 else other_way[t]) for t in range(16)]
        for z in range(8)
        for c in range(2)
    ]
    core = (lax.axis_index("dp") % 2).astype(jnp.int32).reshape(1)

    def tiles(*lead):
        return pltpu.VMEM((*lead, 8, LANES), f32)

    merged_out, send = call(
        first_out,
        (pltpu.VMEM(out_shape, bf16), tiles(16, 2)),
        [far] * 3,
        (grad_out, error_out, distant(warm_out.T)),
        [
            pltpu.VMEM((8, out_shape[1]), f32),
            pltpu.VMEM(out_shape, bf16),
            pltpu.VMEM(out_shape, bf16),
            pltpu.SemaphoreType.DMA((2, OUT_CHUNKS)),
            pltpu.SemaphoreType.DMA,
        ],
        2.6,
    )
    received = exchange(send, "dp", replicas)
    merged_kv, stored, keep_kv, give_kv = call(
        first_kv,
        (pltpu.HBM(kv_shape, bf16), pltpu.HBM(out_shape, bf16), tiles(16, 2), tiles(16, 2)),
        [scalar] + [far] * 3 + [whole],
        (core, grad_kv, error_kv, distant(warm_kv.T), resident(merged_out)),
        [
            pltpu.VMEM((8, kv_shape[1]), f32),
            pltpu.VMEM(kv_shape, bf16),
            pltpu.VMEM(kv_shape, bf16),
            pltpu.VMEM(kv_shape, bf16),
            pltpu.SemaphoreType.DMA((2, KV_CHUNKS)),
            pltpu.SemaphoreType.DMA((KV_CHUNKS,)),
            pltpu.SemaphoreType.DMA,
            pltpu.SemaphoreType.DMA,
        ],
        2.6,
    )
    give_out, sketch_out, terms = call(
        second_give,
        (tiles(16, 1), tiles(2), pltpu.VMEM((32, out_shape[0]), bf16)),
        [scalar] + [whole] * 2,
        (core, resident(received), resident(merged_out)),
        seconds=0.3,
    )
    keep_out, merged_kv = call(
        second_keep,
        (tiles(16, 1), pltpu.HBM(kv_shape, bf16)),
        [scalar] + [whole] * 2 + [far],
        (core, resident(terms), resident(merged_out), distant(merged_kv)),
        seconds=0.2,
        aliases={3: 1},
    )
    kv = keep_kv + lax.ppermute(give_kv, "dp", swap)
    out = keep_out + lax.ppermute(give_out, "dp", swap)
    received = exchange(jnp.concatenate([kv, out], axis=1), ("dp", "tensor"), planes)
    send = call(third, tiles(8, 3), [whole], (resident(received),), seconds=0.1)
    received = exchange(send, "dp", columns)
    send = call(fourth, tiles(16, 3), [whole], (resident(received),), seconds=0.1)
    mine = exchange(send, ("dp", "tensor"), planes)
    other = lax.ppermute(mine, "dp", swap)
    begun = call(
        fifth_mine,
        tiles(),
        [scalar] + [whole] * 2,
        (core, resident(mine), resident(merged_kv)),
        seconds=0.5,
    )
    send = call(
        fifth_other,
        tiles(16),
        [scalar] + [whole] * 3,
        (core, resident(other), resident(merged_kv), resident(begun)),
        seconds=0.5,
    )
    received = exchange(send, "dp", replicas)
    basis, lower, scale = call(
        orthonormal_kv,
        (pltpu.VMEM((8, kv_shape[0]), f32), tiles(8), tiles()),
        [scalar] + [whole] * 2,
        (core, resident(mine), resident(other)),
    )
    factor_out, residual_out = call(
        finish_out,
        (pltpu.HBM((8, out_shape[1]), f32), pltpu.HBM(out_shape, bf16)),
        [scalar] + [whole] * 2 + [far, whole, far],
        (
            core,
            resident(mine),
            resident(other),
            distant(warm_out.T),
            resident(sketch_out),
            distant(stored),
        ),
        [
            pltpu.VMEM(out_shape, bf16),
            pltpu.VMEM(out_shape, bf16),
            pltpu.VMEM((8, out_shape[1]), f32),
            pltpu.VMEM((8, out_shape[1]), f32),
            pltpu.SemaphoreType.DMA((4,)),
            pltpu.SemaphoreType.DMA((4,)),
            pltpu.SemaphoreType.DMA,
            pltpu.SemaphoreType.DMA,
        ],
        2.5,
    )
    factor_kv, residual_kv = call(
        finish_kv,
        (pltpu.HBM((8, kv_shape[1]), f32), pltpu.HBM(kv_shape, bf16)),
        [whole] * 5,
        tuple(resident(value) for value in (received, lower, scale, basis, merged_kv)),
        [
            pltpu.VMEM(kv_shape, bf16),
            pltpu.VMEM((8, kv_shape[1]), f32),
            pltpu.SemaphoreType.DMA((8,)),
            pltpu.SemaphoreType.DMA,
        ],
        2.5,
    )
    return factor_kv.T, factor_out.T, residual_kv[None], residual_out[None]


def solution(mesh):
    placed = (
        P("dp", None, "tensor"),
        P("dp", None, "tensor"),
        P("dp", "tensor", None),
        P("dp", "tensor", None),
        P("tensor", None),
        P(),
    )
    return jax.shard_map(
        per_device,
        mesh=mesh,
        in_specs=placed,
        out_specs=(P("tensor", None), P(), P("dp", None, "tensor"), P("dp", "tensor", None)),
        check_vma=False,
    )
```

```python
import jax
import jax.numpy as jnp
from jax import lax
from jax.experimental import pallas as pl
from jax.experimental.pallas import tpu as pltpu
from jax.sharding import PartitionSpec as P

epsilon = 1e-06
f32 = jnp.float32
bf16 = jnp.bfloat16
LANES = 128
KV_CHUNKS = 4
OUT_CHUNKS = 4
limit = pltpu.CompilerParams(vmem_limit_bytes=24 * 1024 * 1024)
whole = pl.BlockSpec(memory_space=pltpu.VMEM)


def resident(value):
    return pltpu.with_memory_space_constraint(value, pltpu.VMEM)


def distant(value):
    return pltpu.with_memory_space_constraint(value, pltpu.HBM)


def merge(grad, error):
    return (grad.astype(f32) + error.astype(f32)).astype(bf16)


def split(value):
    high = value.astype(bf16)
    low = (value - high.astype(f32)).astype(bf16)
    return high, low


def row(tile, index):
    return jnp.broadcast_to(tile[index : index + 1, :], tile.shape)


def gram_columns(tiles):
    sums = [None] * 8
    for tile in tiles:
        for j in range(8):
            product = tile * row(tile, j)
            sums[j] = product if sums[j] is None else sums[j] + product
    return [
        jnp.broadcast_to(jnp.sum(total, axis=1, keepdims=True), (8, LANES)) for total in sums
    ]


def cholesky(columns):
    place = lax.broadcasted_iota(jnp.int32, (8, LANES), 0)
    columns = [
        column + jnp.where(place == j, epsilon, 0.0).astype(f32)
        for j, column in enumerate(columns)
    ]
    steps = []
    scale = jnp.zeros((8, LANES), f32)
    for j in range(8):
        inverse = lax.rsqrt(jnp.maximum(row(columns[j], j), epsilon))
        lower = jnp.where(place > j, columns[j] * inverse, 0.0)
        for k in range(j + 1, 8):
            columns[k] = columns[k] - lower * row(lower, k)
        steps.append(lower * inverse)
        scale = jnp.where(place == j, inverse, scale)
    return steps, scale


def substitute(tile, steps, scale):
    for j in range(7):
        tile = tile - steps[j] * row(tile, j)
    return tile * scale


def left_terms(value):
    high, low = split(value)
    high, low = high.astype(f32), low.astype(f32)
    return jnp.concatenate([high, low, high, jnp.zeros_like(high)], axis=0).T.astype(bf16)


def right_terms(value):
    high, low = split(value)
    high, low = high.astype(f32), low.astype(f32)
    return jnp.concatenate([high, high, low, jnp.zeros_like(high)], axis=0).astype(bf16)


def block(index, size):
    start = index * size
    return pl.ds(start if isinstance(index, int) else pl.multiple_of(start, size), size)


def first_out(grad, error, warm, merged_out, send, warm_near, near, far_, arrived, warm_arrived):
    wide = near.shape[1] // OUT_CHUNKS

    def copies(c):
        part = block(c, wide)
        return [
            pltpu.make_async_copy(source.at[:, part], target.at[:, part], arrived.at[k, c])
            for k, (source, target) in enumerate(((grad, near), (error, far_)))
        ]

    warm_copy = pltpu.make_async_copy(warm, warm_near, warm_arrived)
    warm_copy.start()

    @pl.loop(0, OUT_CHUNKS)
    def _(c):
        for copy in copies(c):
            copy.start()

    warm_copy.wait()

    def step(c, total):
        for copy in copies(c):
            copy.wait()
        part = block(c, wide)
        merged = merge(near[:, part], far_[:, part])
        merged_out[:, part] = merged
        return total + lax.dot_general(
            warm_near[:, part].astype(bf16),
            merged,
            (((1,), (1,)), ((), ())),
            preferred_element_type=f32,
        )

    total = lax.fori_loop(0, OUT_CHUNKS, step, jnp.zeros((8, near.shape[0]), f32))
    for d in range(16):
        for k in range(2):
            send[d, k] = total[:, k * LANES : (k + 1) * LANES]


def first_kv(core, grad, error, warm, merged_out, merged_kv, stored_out, keep, give, warm_near,
             near, far_, done, arrived, sent, warm_arrived, out_sent):
    rows = near.shape[0] // KV_CHUNKS

    def copies(c):
        part = block(c, rows)
        return [
            pltpu.make_async_copy(source.at[part], target.at[part], arrived.at[k, c])
            for k, (source, target) in enumerate(((grad, near), (error, far_)))
        ]

    def leaving(c):
        part = block(c, rows)
        return pltpu.make_async_copy(done.at[part], merged_kv.at[part], sent.at[c])

    warm_copy = pltpu.make_async_copy(warm, warm_near, warm_arrived)
    warm_copy.start()

    @pl.loop(0, KV_CHUNKS)
    def _(c):
        for copy in copies(c):
            copy.start()

    warm_copy.wait()
    out_copy = pltpu.make_async_copy(merged_out, stored_out, out_sent)
    out_copy.start()
    right = warm_near[...].astype(bf16)
    even = jnp.full((8, LANES), core[0], jnp.int32) == 0
    for c in range(KV_CHUNKS):
        for copy in copies(c):
            copy.wait()
        part = block(c, rows)
        merged = merge(near[part, :], far_[part, :])
        done[part, :] = merged
        leaving(c).start()
        sketch = lax.dot_general(
            right, merged, (((1,), (1,)), ((), ())), preferred_element_type=f32
        )
        for t in range(4):
            for k in range(2):
                first = (4 * t + k) * LANES
                zero = sketch[:, first : first + LANES]
                one = sketch[:, first + 2 * LANES : first + 3 * LANES]
                keep[4 * c + t, k] = jnp.where(even, zero, one)
                give[4 * c + t, k] = jnp.where(even, one, zero)

    out_copy.wait()

    @pl.loop(0, KV_CHUNKS)
    def _(c):
        leaving(c).wait()


def total_of(received, index):
    value = received[0, index]
    for d in range(1, received.shape[0]):
        value = value + received[d, index]
    return value


def half_factor(left, merged_out, half, target):
    wide = merged_out.shape[1] // 4
    for c in range(2):
        part = pl.ds(pl.multiple_of((2 * half + c) * wide, wide), wide)
        terms = jnp.dot(left, merged_out[:, part], preferred_element_type=f32)
        total = terms[:8] + (terms[8:16] + terms[16:24])
        for t in range(8):
            target[8 * c + t, 0] = total[:, t * LANES : (t + 1) * LANES]


def second_give(core, received, merged_out, give, sketch_out, terms):
    tiles = [total_of(received, k) for k in range(2)]
    sketch_out[0] = tiles[0]
    sketch_out[1] = tiles[1]
    value = jnp.concatenate(tiles, axis=1)
    high = value.astype(bf16)
    middle, low = split(value - high.astype(f32))
    left = jnp.concatenate(
        [part.astype(f32) for part in (high, middle, low, jnp.zeros_like(low))], axis=0
    ).astype(bf16)
    terms[...] = left
    half_factor(left, merged_out, 1 - core[0], give)


def second_keep(core, terms, merged_out, merged_kv, keep, same_kv):
    del merged_kv, same_kv
    half_factor(terms[...], merged_out, core[0], keep)


def third(received, send):
    tiles = [total_of(received, k) for k in range(3)]
    for z in range(8):
        for k in range(3):
            send[z, k] = tiles[k]


def fourth(received, send):
    tiles = [total_of(received, k) for k in range(3)]
    for t in range(16):
        for k in range(3):
            send[t, k] = tiles[k]


def in_order(core, mine, other):
    even = jnp.full((8, LANES), core[0], jnp.int32) == 0
    tiles = []
    for t in range(16):
        for k in range(2):
            tiles.append(jnp.where(even, mine[t, k], other[t, k]))
        for k in range(2):
            tiles.append(jnp.where(even, other[t, k], mine[t, k]))
    return tiles


def partial_factor(core, which, tiles, merged_kv):
    base = lax.rem(core[0] + which, 2) * 256
    term = jnp.zeros((16, LANES), f32)
    for t in range(16):
        high, low = split(jnp.concatenate([tiles[t, 0], tiles[t, 1]], axis=1))
        left = jnp.concatenate([high.astype(f32), low.astype(f32)], axis=0).astype(bf16)
        rows = pl.ds(pl.multiple_of(t * 512 + base, 256), 256)
        term = term + jnp.dot(left, merged_kv[rows, :], preferred_element_type=f32)
    return term[:8] + term[8:]


def fifth_mine(core, mine, merged_kv, term):
    term[...] = partial_factor(core, 0, mine, merged_kv)


def fifth_other(core, other, merged_kv, begun, send):
    term = begun[...] + partial_factor(core, 1, other, merged_kv)
    for d in range(16):
        send[d] = term


def orthonormal_kv(core, mine, other, basis, lower, scale):
    tiles = in_order(core, mine, other)
    steps, inverse = cholesky(gram_columns(tiles))
    for j in range(8):
        lower[j] = steps[j]
    scale[...] = inverse
    for k, tile in enumerate(tiles):
        basis[:, k * LANES : (k + 1) * LANES] = substitute(tile, steps, inverse)


def finish_out(core, mine, other, warm, sketch_out, merged_out, factor, residual, near, done,
               factor_near, warm_near, arrived, sent, factor_sent, warm_arrived):
    wide = done.shape[1] // 4

    def arriving(c):
        part = block(c, wide)
        return pltpu.make_async_copy(merged_out.at[:, part], near.at[:, part], arrived.at[c])

    def leaving(c):
        part = block(c, wide)
        return pltpu.make_async_copy(done.at[:, part], residual.at[:, part], sent.at[c])

    warm_copy = pltpu.make_async_copy(warm, warm_near, warm_arrived)
    warm_copy.start()

    @pl.loop(0, 4)
    def _(c):
        arriving(c).start()

    even = jnp.full((8, LANES), core[0], jnp.int32) == 0
    values = [jnp.where(even, mine[t, 2], other[t, 2]) for t in range(16)]
    values += [jnp.where(even, other[t, 2], mine[t, 2]) for t in range(16)]
    warm_copy.wait()
    sums = [jnp.zeros((8, LANES), f32)] * 8
    for k, tile in enumerate(values):
        right = warm_near[:, k * LANES : (k + 1) * LANES].astype(bf16).astype(f32)
        for j in range(8):
            sums[j] = sums[j] + right * row(tile, j)
    steps, scale = cholesky(
        [jnp.broadcast_to(jnp.sum(total, axis=1, keepdims=True), (8, LANES)) for total in sums]
    )
    basis = [substitute(sketch_out[k], steps, scale) for k in range(2)]
    left = left_terms(jnp.concatenate(basis, axis=1))
    values = [substitute(tile, steps, scale) * (1.0 / 16.0) for tile in values]
    for k, value in enumerate(values):
        factor_near[:, k * LANES : (k + 1) * LANES] = value
    factor_copy = pltpu.make_async_copy(factor_near, factor, factor_sent)
    factor_copy.start()
    for c in range(4):
        right = right_terms(jnp.concatenate(values[8 * c : 8 * c + 8], axis=1))
        part = block(c, wide)
        approx = jnp.dot(left, right, preferred_element_type=f32)
        arriving(c).wait()
        done[:, part] = (near[:, part].astype(f32) - approx).astype(bf16)
        leaving(c).start()

    @pl.loop(0, 4)
    def _(c):
        leaving(c).wait()

    factor_copy.wait()


def finish_kv(received, lower, scale, basis, merged_kv, factor, residual, done, factor_near, sent,
              factor_sent):
    rows = 1024

    def leaving(c):
        part = block(c, rows)
        return pltpu.make_async_copy(done.at[part], residual.at[part], sent.at[c])

    value = received[0]
    for d in range(1, 16):
        value = value + received[d]
    value = substitute(value, [lower[j] for j in range(8)], scale[...]) * (1.0 / 16.0)
    factor_near[...] = value
    factor_copy = pltpu.make_async_copy(factor_near, factor, factor_sent)
    factor_copy.start()
    right = right_terms(value)
    for c in range(8):
        part = block(c, rows)
        left = left_terms(basis[:, part])
        approx = jnp.dot(left, right, preferred_element_type=f32)
        done[part, :] = (merged_kv[part, :].astype(f32) - approx).astype(bf16)
        leaving(c).start()

    @pl.loop(0, 8)
    def _(c):
        leaving(c).wait()

    factor_copy.wait()


def exchange(value, axis, groups=None):
    return lax.all_to_all(value, axis, 0, 0, axis_index_groups=groups)


def call(kernel, outs, ins, args, scratch=(), seconds=1.0, aliases=None):
    return pl.pallas_call(
        kernel,
        out_shape=outs,
        in_specs=ins,
        out_specs=jax.tree.map(
            lambda out: far if isinstance(out, pl.MemoryRef) and out.memory_space == pltpu.HBM else whole,
            outs,
            is_leaf=lambda out: not isinstance(out, tuple),
        ),
        scratch_shapes=list(scratch),
        input_output_aliases=aliases or {},
        compiler_params=limit,
        cost_estimate=pl.CostEstimate(
            flops=0, bytes_accessed=int(seconds * 2_000_000), transcendentals=0
        ),
        name=kernel.__name__,
    )(*args)


far = pl.BlockSpec(memory_space=pltpu.HBM)
scalar = pl.BlockSpec(memory_space=pltpu.SMEM)


def per_device(grad_kv, error_kv, grad_out, error_out, warm_kv, warm_out):
    grad_kv, error_kv, grad_out, error_out = (
        distant(value[0]) for value in (grad_kv, error_kv, grad_out, error_out)
    )
    kv_shape, out_shape = grad_kv.shape, grad_out.shape
    columns = [[2 * z + c for z in reversed(range(8))] for c in range(2)]
    replicas = [[15 - d for d in range(16)]]
    swap = [(d, d ^ 1) for d in range(16)]
    other_way = [15 - t for t in range(16)]
    planes = [
        [(2 * z + c) * 16 + other_way[t] for t in range(16)]
        for z in range(8)
        for c in range(2)
    ]
    core = (lax.axis_index("dp") % 2).astype(jnp.int32).reshape(1)

    def tiles(*lead):
        return pltpu.VMEM((*lead, 8, LANES), f32)

    merged_out, send = call(
        first_out,
        (pltpu.VMEM(out_shape, bf16), tiles(16, 2)),
        [far] * 3,
        (grad_out, error_out, distant(warm_out.T)),
        [
            pltpu.VMEM((8, out_shape[1]), f32),
            pltpu.VMEM(out_shape, bf16),
            pltpu.VMEM(out_shape, bf16),
            pltpu.SemaphoreType.DMA((2, OUT_CHUNKS)),
            pltpu.SemaphoreType.DMA,
        ],
        2.6,
    )
    received = exchange(send, "dp", replicas)
    merged_kv, stored, keep_kv, give_kv = call(
        first_kv,
        (pltpu.HBM(kv_shape, bf16), pltpu.HBM(out_shape, bf16), tiles(16, 2), tiles(16, 2)),
        [scalar] + [far] * 3 + [whole],
        (core, grad_kv, error_kv, distant(warm_kv.T), resident(merged_out)),
        [
            pltpu.VMEM((8, kv_shape[1]), f32),
            pltpu.VMEM(kv_shape, bf16),
            pltpu.VMEM(kv_shape, bf16),
            pltpu.VMEM(kv_shape, bf16),
            pltpu.SemaphoreType.DMA((2, KV_CHUNKS)),
            pltpu.SemaphoreType.DMA((KV_CHUNKS,)),
            pltpu.SemaphoreType.DMA,
            pltpu.SemaphoreType.DMA,
        ],
        2.6,
    )
    give_out, sketch_out, terms = call(
        second_give,
        (tiles(16, 1), tiles(2), pltpu.VMEM((32, out_shape[0]), bf16)),
        [scalar] + [whole] * 2,
        (core, resident(received), resident(merged_out)),
        seconds=0.3,
    )
    keep_out, merged_kv = call(
        second_keep,
        (tiles(16, 1), pltpu.HBM(kv_shape, bf16)),
        [scalar] + [whole] * 2 + [far],
        (core, resident(terms), resident(merged_out), distant(merged_kv)),
        seconds=0.2,
        aliases={3: 1},
    )
    kv = keep_kv + lax.ppermute(give_kv, "dp", swap)
    out = keep_out + lax.ppermute(give_out, "dp", swap)
    received = exchange(jnp.concatenate([kv, out], axis=1), ("dp", "tensor"), planes)
    send = call(third, tiles(8, 3), [whole], (resident(received),), seconds=0.1)
    received = exchange(send, "dp", columns)
    send = call(fourth, tiles(16, 3), [whole], (resident(received),), seconds=0.1)
    mine = exchange(send, ("dp", "tensor"), planes)
    other = lax.ppermute(mine, "dp", swap)
    begun = call(
        fifth_mine,
        tiles(),
        [scalar] + [whole] * 2,
        (core, resident(mine), resident(merged_kv)),
        seconds=0.5,
    )
    send = call(
        fifth_other,
        tiles(16),
        [scalar] + [whole] * 3,
        (core, resident(other), resident(merged_kv), resident(begun)),
        seconds=0.5,
    )
    received = exchange(send, "dp", replicas)
    basis, lower, scale = call(
        orthonormal_kv,
        (pltpu.VMEM((8, kv_shape[0]), f32), tiles(8), tiles()),
        [scalar] + [whole] * 2,
        (core, resident(mine), resident(other)),
    )
    factor_out, residual_out = call(
        finish_out,
        (pltpu.HBM((8, out_shape[1]), f32), pltpu.HBM(out_shape, bf16)),
        [scalar] + [whole] * 2 + [far, whole, far],
        (
            core,
            resident(mine),
            resident(other),
            distant(warm_out.T),
            resident(sketch_out),
            distant(stored),
        ),
        [
            pltpu.VMEM(out_shape, bf16),
            pltpu.VMEM(out_shape, bf16),
            pltpu.VMEM((8, out_shape[1]), f32),
            pltpu.VMEM((8, out_shape[1]), f32),
            pltpu.SemaphoreType.DMA((4,)),
            pltpu.SemaphoreType.DMA((4,)),
            pltpu.SemaphoreType.DMA,
            pltpu.SemaphoreType.DMA,
        ],
        2.5,
    )
    factor_kv, residual_kv = call(
        finish_kv,
        (pltpu.HBM((8, kv_shape[1]), f32), pltpu.HBM(kv_shape, bf16)),
        [whole] * 5,
        tuple(resident(value) for value in (received, lower, scale, basis, merged_kv)),
        [
            pltpu.VMEM(kv_shape, bf16),
            pltpu.VMEM((8, kv_shape[1]), f32),
            pltpu.SemaphoreType.DMA((8,)),
            pltpu.SemaphoreType.DMA,
        ],
        2.5,
    )
    return factor_kv.T, factor_out.T, residual_kv[None], residual_out[None]


def solution(mesh):
    placed = (
        P("dp", None, "tensor"),
        P("dp", None, "tensor"),
        P("dp", "tensor", None),
        P("dp", "tensor", None),
        P("tensor", None),
        P(),
    )
    return jax.shard_map(
        per_device,
        mesh=mesh,
        in_specs=placed,
        out_specs=(P("tensor", None), P(), P("dp", None, "tensor"), P("dp", "tensor", None)),
        check_vma=False,
    )
```

```python
import jax
import jax.numpy as jnp
from jax import lax
from jax.experimental import pallas as pl
from jax.experimental.pallas import tpu as pltpu
from jax.sharding import PartitionSpec as P

epsilon = 1e-06
f32 = jnp.float32
bf16 = jnp.bfloat16
LANES = 128
KV_CHUNKS = 4
OUT_CHUNKS = 4
limit = pltpu.CompilerParams(vmem_limit_bytes=24 * 1024 * 1024)
whole = pl.BlockSpec(memory_space=pltpu.VMEM)


def resident(value):
    return pltpu.with_memory_space_constraint(value, pltpu.VMEM)


def distant(value):
    return pltpu.with_memory_space_constraint(value, pltpu.HBM)


def merge(grad, error):
    return (grad.astype(f32) + error.astype(f32)).astype(bf16)


def split(value):
    high = value.astype(bf16)
    low = (value - high.astype(f32)).astype(bf16)
    return high, low


def row(tile, index):
    return jnp.broadcast_to(tile[index : index + 1, :], tile.shape)


def gram_columns(tiles):
    sums = [None] * 8
    for tile in tiles:
        for j in range(8):
            product = tile * row(tile, j)
            sums[j] = product if sums[j] is None else sums[j] + product
    return [
        jnp.broadcast_to(jnp.sum(total, axis=1, keepdims=True), (8, LANES)) for total in sums
    ]


def cholesky(columns):
    place = lax.broadcasted_iota(jnp.int32, (8, LANES), 0)
    columns = [
        column + jnp.where(place == j, epsilon, 0.0).astype(f32)
        for j, column in enumerate(columns)
    ]
    steps = []
    scale = jnp.zeros((8, LANES), f32)
    for j in range(8):
        inverse = lax.rsqrt(jnp.maximum(row(columns[j], j), epsilon))
        lower = jnp.where(place > j, columns[j] * inverse, 0.0)
        for k in range(j + 1, 8):
            columns[k] = columns[k] - lower * row(lower, k)
        steps.append(lower * inverse)
        scale = jnp.where(place == j, inverse, scale)
    return steps, scale


def substitute(tile, steps, scale):
    for j in range(7):
        tile = tile - steps[j] * row(tile, j)
    return tile * scale


def left_terms(value):
    high, low = split(value)
    high, low = high.astype(f32), low.astype(f32)
    return jnp.concatenate([high, low, high, jnp.zeros_like(high)], axis=0).T.astype(bf16)


def right_terms(value):
    high, low = split(value)
    high, low = high.astype(f32), low.astype(f32)
    return jnp.concatenate([high, high, low, jnp.zeros_like(high)], axis=0).astype(bf16)


def block(index, size):
    start = index * size
    return pl.ds(start if isinstance(index, int) else pl.multiple_of(start, size), size)


def first_out(grad, error, warm, merged_out, send, warm_near, near, far_, arrived, warm_arrived):
    wide = near.shape[1] // OUT_CHUNKS

    def copies(c):
        part = block(c, wide)
        return [
            pltpu.make_async_copy(source.at[:, part], target.at[:, part], arrived.at[k, c])
            for k, (source, target) in enumerate(((grad, near), (error, far_)))
        ]

    warm_copy = pltpu.make_async_copy(warm, warm_near, warm_arrived)
    warm_copy.start()

    @pl.loop(0, OUT_CHUNKS)
    def _(c):
        for copy in copies(c):
            copy.start()

    warm_copy.wait()

    def step(c, total):
        for copy in copies(c):
            copy.wait()
        part = block(c, wide)
        merged = merge(near[:, part], far_[:, part])
        merged_out[:, part] = merged
        return total + lax.dot_general(
            warm_near[:, part].astype(bf16),
            merged,
            (((1,), (1,)), ((), ())),
            preferred_element_type=f32,
        )

    total = lax.fori_loop(0, OUT_CHUNKS, step, jnp.zeros((8, near.shape[0]), f32))
    for d in range(16):
        for k in range(2):
            send[d, k] = total[:, k * LANES : (k + 1) * LANES]


def first_kv(core, grad, error, warm, merged_out, merged_kv, stored_out, keep, give, warm_near,
             near, far_, done, arrived, sent, warm_arrived, out_sent):
    rows = near.shape[0] // KV_CHUNKS

    def copies(c):
        part = block(c, rows)
        return [
            pltpu.make_async_copy(source.at[part], target.at[part], arrived.at[k, c])
            for k, (source, target) in enumerate(((grad, near), (error, far_)))
        ]

    def leaving(c):
        part = block(c, rows)
        return pltpu.make_async_copy(done.at[part], merged_kv.at[part], sent.at[c])

    warm_copy = pltpu.make_async_copy(warm, warm_near, warm_arrived)
    warm_copy.start()

    @pl.loop(0, KV_CHUNKS)
    def _(c):
        for copy in copies(c):
            copy.start()

    warm_copy.wait()
    out_copy = pltpu.make_async_copy(merged_out, stored_out, out_sent)
    out_copy.start()
    right = warm_near[...].astype(bf16)
    even = jnp.full((8, LANES), core[0], jnp.int32) == 0
    for c in range(KV_CHUNKS):
        for copy in copies(c):
            copy.wait()
        part = block(c, rows)
        merged = merge(near[part, :], far_[part, :])
        done[part, :] = merged
        leaving(c).start()
        sketch = lax.dot_general(
            right, merged, (((1,), (1,)), ((), ())), preferred_element_type=f32
        )
        for t in range(4):
            for k in range(2):
                first = (4 * t + k) * LANES
                zero = sketch[:, first : first + LANES]
                one = sketch[:, first + 2 * LANES : first + 3 * LANES]
                keep[4 * c + t, k] = jnp.where(even, zero, one)
                give[4 * c + t, k] = jnp.where(even, one, zero)

    out_copy.wait()

    @pl.loop(0, KV_CHUNKS)
    def _(c):
        leaving(c).wait()


def total_of(received, index):
    value = received[0, index]
    for d in range(1, received.shape[0]):
        value = value + received[d, index]
    return value


def half_factor(left, merged_out, half, target):
    wide = merged_out.shape[1] // 4
    for c in range(2):
        part = pl.ds(pl.multiple_of((2 * half + c) * wide, wide), wide)
        terms = jnp.dot(left, merged_out[:, part], preferred_element_type=f32)
        total = terms[:8] + (terms[8:16] + terms[16:24])
        for t in range(8):
            target[8 * c + t, 0] = total[:, t * LANES : (t + 1) * LANES]


def second_give(core, received, merged_out, give, sketch_out, terms):
    tiles = [total_of(received, k) for k in range(2)]
    sketch_out[0] = tiles[0]
    sketch_out[1] = tiles[1]
    value = jnp.concatenate(tiles, axis=1)
    high = value.astype(bf16)
    middle, low = split(value - high.astype(f32))
    left = jnp.concatenate(
        [part.astype(f32) for part in (high, middle, low, jnp.zeros_like(low))], axis=0
    ).astype(bf16)
    terms[...] = left
    half_factor(left, merged_out, 1 - core[0], give)


def second_keep(core, terms, merged_out, merged_kv, keep, same_kv):
    del merged_kv, same_kv
    half_factor(terms[...], merged_out, core[0], keep)


def third(received, send):
    tiles = [total_of(received, k) for k in range(3)]
    for z in range(8):
        for k in range(3):
            send[z, k] = tiles[k]


def fourth(received, send):
    tiles = [total_of(received, k) for k in range(3)]
    for t in range(16):
        for k in range(3):
            send[t, k] = tiles[k]


def in_order(core, mine, other):
    even = jnp.full((8, LANES), core[0], jnp.int32) == 0
    tiles = []
    for t in range(16):
        for k in range(2):
            tiles.append(jnp.where(even, mine[t, k], other[t, k]))
        for k in range(2):
            tiles.append(jnp.where(even, other[t, k], mine[t, k]))
    return tiles


def partial_factor(core, which, tiles, merged_kv):
    base = lax.rem(core[0] + which, 2) * 256
    term = jnp.zeros((16, LANES), f32)
    for t in range(16):
        high, low = split(jnp.concatenate([tiles[t, 0], tiles[t, 1]], axis=1))
        left = jnp.concatenate([high.astype(f32), low.astype(f32)], axis=0).astype(bf16)
        rows = pl.ds(pl.multiple_of(t * 512 + base, 256), 256)
        term = term + jnp.dot(left, merged_kv[rows, :], preferred_element_type=f32)
    return term[:8] + term[8:]


def fifth_mine(core, mine, merged_kv, term):
    term[...] = partial_factor(core, 0, mine, merged_kv)


def fifth_other(core, other, merged_kv, begun, send):
    term = begun[...] + partial_factor(core, 1, other, merged_kv)
    for d in range(16):
        send[d] = term


def orthonormal_kv(core, mine, other, basis, lower, scale):
    tiles = in_order(core, mine, other)
    steps, inverse = cholesky(gram_columns(tiles))
    for j in range(8):
        lower[j] = steps[j]
    scale[...] = inverse
    for k, tile in enumerate(tiles):
        basis[:, k * LANES : (k + 1) * LANES] = substitute(tile, steps, inverse)


def finish_out(core, mine, other, warm, sketch_out, merged_out, factor, residual, near, done,
               factor_near, warm_near, arrived, sent, factor_sent, warm_arrived):
    wide = done.shape[1] // 4

    def arriving(c):
        part = block(c, wide)
        return pltpu.make_async_copy(merged_out.at[:, part], near.at[:, part], arrived.at[c])

    def leaving(c):
        part = block(c, wide)
        return pltpu.make_async_copy(done.at[:, part], residual.at[:, part], sent.at[c])

    warm_copy = pltpu.make_async_copy(warm, warm_near, warm_arrived)
    warm_copy.start()

    @pl.loop(0, 4)
    def _(c):
        arriving(c).start()

    even = jnp.full((8, LANES), core[0], jnp.int32) == 0
    values = [jnp.where(even, mine[t, 2], other[t, 2]) for t in range(16)]
    values += [jnp.where(even, other[t, 2], mine[t, 2]) for t in range(16)]
    warm_copy.wait()
    sums = [jnp.zeros((8, LANES), f32)] * 8
    for k, tile in enumerate(values):
        right = warm_near[:, k * LANES : (k + 1) * LANES].astype(bf16).astype(f32)
        for j in range(8):
            sums[j] = sums[j] + right * row(tile, j)
    steps, scale = cholesky(
        [jnp.broadcast_to(jnp.sum(total, axis=1, keepdims=True), (8, LANES)) for total in sums]
    )
    basis = [substitute(sketch_out[k], steps, scale) for k in range(2)]
    left = left_terms(jnp.concatenate(basis, axis=1))
    values = [substitute(tile, steps, scale) * (1.0 / 16.0) for tile in values]
    for k, value in enumerate(values):
        factor_near[:, k * LANES : (k + 1) * LANES] = value
    factor_copy = pltpu.make_async_copy(factor_near, factor, factor_sent)
    factor_copy.start()
    for c in range(4):
        right = right_terms(jnp.concatenate(values[8 * c : 8 * c + 8], axis=1))
        part = block(c, wide)
        approx = jnp.dot(left, right, preferred_element_type=f32)
        arriving(c).wait()
        done[:, part] = (near[:, part].astype(f32) - approx).astype(bf16)
        leaving(c).start()

    @pl.loop(0, 4)
    def _(c):
        leaving(c).wait()

    factor_copy.wait()


def finish_kv(received, lower, scale, basis, merged_kv, factor, residual, done, factor_near, sent,
              factor_sent):
    rows = 1024

    def leaving(c):
        part = block(c, rows)
        return pltpu.make_async_copy(done.at[part], residual.at[part], sent.at[c])

    value = received[0]
    for d in range(1, 16):
        value = value + received[d]
    value = substitute(value, [lower[j] for j in range(8)], scale[...]) * (1.0 / 16.0)
    factor_near[...] = value
    factor_copy = pltpu.make_async_copy(factor_near, factor, factor_sent)
    factor_copy.start()
    right = right_terms(value)
    for c in range(8):
        part = block(c, rows)
        left = left_terms(basis[:, part])
        approx = jnp.dot(left, right, preferred_element_type=f32)
        done[part, :] = (merged_kv[part, :].astype(f32) - approx).astype(bf16)
        leaving(c).start()

    @pl.loop(0, 8)
    def _(c):
        leaving(c).wait()

    factor_copy.wait()


def exchange(value, axis, groups=None):
    return lax.all_to_all(value, axis, 0, 0, axis_index_groups=groups)


def call(kernel, outs, ins, args, scratch=(), seconds=1.0, aliases=None):
    return pl.pallas_call(
        kernel,
        out_shape=outs,
        in_specs=ins,
        out_specs=jax.tree.map(
            lambda out: far if isinstance(out, pl.MemoryRef) and out.memory_space == pltpu.HBM else whole,
            outs,
            is_leaf=lambda out: not isinstance(out, tuple),
        ),
        scratch_shapes=list(scratch),
        input_output_aliases=aliases or {},
        compiler_params=limit,
        cost_estimate=pl.CostEstimate(
            flops=0, bytes_accessed=int(seconds * 2_000_000), transcendentals=0
        ),
        name=kernel.__name__,
    )(*args)


far = pl.BlockSpec(memory_space=pltpu.HBM)
scalar = pl.BlockSpec(memory_space=pltpu.SMEM)


def per_device(grad_kv, error_kv, grad_out, error_out, warm_kv, warm_out):
    grad_kv, error_kv, grad_out, error_out = (
        distant(value[0]) for value in (grad_kv, error_kv, grad_out, error_out)
    )
    kv_shape, out_shape = grad_kv.shape, grad_out.shape
    columns = [[2 * z + c for z in [6, 7, 5, 4, 3, 2, 1, 0]] for c in range(2)]
    replicas = [[13, 15, 14, 12, 11, 10, 9, 8, 7, 6, 5, 4, 3, 2, 1, 0]]
    swap = [(d, d ^ 1) for d in range(16)]
    other_way = [10, 15, 14, 13, 12, 11, 9, 8, 7, 6, 5, 4, 3, 2, 1, 0]
    planes = [
        [(2 * z + c) * 16 + other_way[t] for t in range(16)]
        for z in range(8)
        for c in range(2)
    ]
    core = (lax.axis_index("dp") % 2).astype(jnp.int32).reshape(1)

    def tiles(*lead):
        return pltpu.VMEM((*lead, 8, LANES), f32)

    merged_out, send = call(
        first_out,
        (pltpu.VMEM(out_shape, bf16), tiles(16, 2)),
        [far] * 3,
        (grad_out, error_out, distant(warm_out.T)),
        [
            pltpu.VMEM((8, out_shape[1]), f32),
            pltpu.VMEM(out_shape, bf16),
            pltpu.VMEM(out_shape, bf16),
            pltpu.SemaphoreType.DMA((2, OUT_CHUNKS)),
            pltpu.SemaphoreType.DMA,
        ],
        2.6,
    )
    received = exchange(send, "dp", replicas)
    merged_kv, stored, keep_kv, give_kv = call(
        first_kv,
        (pltpu.HBM(kv_shape, bf16), pltpu.HBM(out_shape, bf16), tiles(16, 2), tiles(16, 2)),
        [scalar] + [far] * 3 + [whole],
        (core, grad_kv, error_kv, distant(warm_kv.T), resident(merged_out)),
        [
            pltpu.VMEM((8, kv_shape[1]), f32),
            pltpu.VMEM(kv_shape, bf16),
            pltpu.VMEM(kv_shape, bf16),
            pltpu.VMEM(kv_shape, bf16),
            pltpu.SemaphoreType.DMA((2, KV_CHUNKS)),
            pltpu.SemaphoreType.DMA((KV_CHUNKS,)),
            pltpu.SemaphoreType.DMA,
            pltpu.SemaphoreType.DMA,
        ],
        2.6,
    )
    give_out, sketch_out, terms = call(
        second_give,
        (tiles(16, 1), tiles(2), pltpu.VMEM((32, out_shape[0]), bf16)),
        [scalar] + [whole] * 2,
        (core, resident(received), resident(merged_out)),
        seconds=0.3,
    )
    keep_out, merged_kv = call(
        second_keep,
        (tiles(16, 1), pltpu.HBM(kv_shape, bf16)),
        [scalar] + [whole] * 2 + [far],
        (core, resident(terms), resident(merged_out), distant(merged_kv)),
        seconds=0.2,
        aliases={3: 1},
    )
    kv = keep_kv + lax.ppermute(give_kv, "dp", swap)
    out = keep_out + lax.ppermute(give_out, "dp", swap)
    received = exchange(jnp.concatenate([kv, out], axis=1), ("dp", "tensor"), planes)
    send = call(third, tiles(8, 3), [whole], (resident(received),), seconds=0.1)
    received = exchange(send, "dp", columns)
    send = call(fourth, tiles(16, 3), [whole], (resident(received),), seconds=0.1)
    mine = exchange(send, ("dp", "tensor"), planes)
    other = lax.ppermute(mine, "dp", swap)
    begun = call(
        fifth_mine,
        tiles(),
        [scalar] + [whole] * 2,
        (core, resident(mine), resident(merged_kv)),
        seconds=0.5,
    )
    send = call(
        fifth_other,
        tiles(16),
        [scalar] + [whole] * 3,
        (core, resident(other), resident(merged_kv), resident(begun)),
        seconds=0.5,
    )
    received = exchange(send, "dp", replicas)
    basis, lower, scale = call(
        orthonormal_kv,
        (pltpu.VMEM((8, kv_shape[0]), f32), tiles(8), tiles()),
        [scalar] + [whole] * 2,
        (core, resident(mine), resident(other)),
    )
    factor_out, residual_out = call(
        finish_out,
        (pltpu.HBM((8, out_shape[1]), f32), pltpu.HBM(out_shape, bf16)),
        [scalar] + [whole] * 2 + [far, whole, far],
        (
            core,
            resident(mine),
            resident(other),
            distant(warm_out.T),
            resident(sketch_out),
            distant(stored),
        ),
        [
            pltpu.VMEM(out_shape, bf16),
            pltpu.VMEM(out_shape, bf16),
            pltpu.VMEM((8, out_shape[1]), f32),
            pltpu.VMEM((8, out_shape[1]), f32),
            pltpu.SemaphoreType.DMA((4,)),
            pltpu.SemaphoreType.DMA((4,)),
            pltpu.SemaphoreType.DMA,
            pltpu.SemaphoreType.DMA,
        ],
        2.5,
    )
    factor_kv, residual_kv = call(
        finish_kv,
        (pltpu.HBM((8, kv_shape[1]), f32), pltpu.HBM(kv_shape, bf16)),
        [whole] * 5,
        tuple(resident(value) for value in (received, lower, scale, basis, merged_kv)),
        [
            pltpu.VMEM(kv_shape, bf16),
            pltpu.VMEM((8, kv_shape[1]), f32),
            pltpu.SemaphoreType.DMA((8,)),
            pltpu.SemaphoreType.DMA,
        ],
        2.5,
    )
    return factor_kv.T, factor_out.T, residual_kv[None], residual_out[None]


def solution(mesh):
    placed = (
        P("dp", None, "tensor"),
        P("dp", None, "tensor"),
        P("dp", "tensor", None),
        P("dp", "tensor", None),
        P("tensor", None),
        P(),
    )
    return jax.shard_map(
        per_device,
        mesh=mesh,
        in_specs=placed,
        out_specs=(P("tensor", None), P(), P("dp", None, "tensor"), P("dp", "tensor", None)),
        check_vma=False,
    )
```

```python
import jax
import jax.numpy as jnp
from jax import lax
from jax.experimental import pallas as pl
from jax.experimental.pallas import tpu as pltpu
from jax.sharding import PartitionSpec as P

epsilon = 1e-06
f32 = jnp.float32
bf16 = jnp.bfloat16
LANES = 128
KV_CHUNKS = 4
OUT_CHUNKS = 4
limit = pltpu.CompilerParams(vmem_limit_bytes=24 * 1024 * 1024)
whole = pl.BlockSpec(memory_space=pltpu.VMEM)


def resident(value):
    return pltpu.with_memory_space_constraint(value, pltpu.VMEM)


def distant(value):
    return pltpu.with_memory_space_constraint(value, pltpu.HBM)


def merge(grad, error):
    return (grad.astype(f32) + error.astype(f32)).astype(bf16)


def split(value):
    high = value.astype(bf16)
    low = (value - high.astype(f32)).astype(bf16)
    return high, low


def row(tile, index):
    return jnp.broadcast_to(tile[index : index + 1, :], tile.shape)


def gram_columns(tiles):
    sums = [None] * 8
    for tile in tiles:
        for j in range(8):
            product = tile * row(tile, j)
            sums[j] = product if sums[j] is None else sums[j] + product
    return [
        jnp.broadcast_to(jnp.sum(total, axis=1, keepdims=True), (8, LANES)) for total in sums
    ]


def cholesky(columns):
    place = lax.broadcasted_iota(jnp.int32, (8, LANES), 0)
    columns = [
        column + jnp.where(place == j, epsilon, 0.0).astype(f32)
        for j, column in enumerate(columns)
    ]
    steps = []
    scale = jnp.zeros((8, LANES), f32)
    for j in range(8):
        inverse = lax.rsqrt(jnp.maximum(row(columns[j], j), epsilon))
        lower = jnp.where(place > j, columns[j] * inverse, 0.0)
        for k in range(j + 1, 8):
            columns[k] = columns[k] - lower * row(lower, k)
        steps.append(lower * inverse)
        scale = jnp.where(place == j, inverse, scale)
    return steps, scale


def substitute(tile, steps, scale):
    for j in range(7):
        tile = tile - steps[j] * row(tile, j)
    return tile * scale


def left_terms(value):
    high, low = split(value)
    high, low = high.astype(f32), low.astype(f32)
    return jnp.concatenate([high, low, high, jnp.zeros_like(high)], axis=0).T.astype(bf16)


def right_terms(value):
    high, low = split(value)
    high, low = high.astype(f32), low.astype(f32)
    return jnp.concatenate([high, high, low, jnp.zeros_like(high)], axis=0).astype(bf16)


def block(index, size):
    start = index * size
    return pl.ds(start if isinstance(index, int) else pl.multiple_of(start, size), size)


def first_out(grad, error, warm, merged_out, send, warm_near, near, far_, arrived, warm_arrived):
    wide = near.shape[1] // OUT_CHUNKS

    def copies(c):
        part = block(c, wide)
        return [
            pltpu.make_async_copy(source.at[:, part], target.at[:, part], arrived.at[k, c])
            for k, (source, target) in enumerate(((grad, near), (error, far_)))
        ]

    warm_copy = pltpu.make_async_copy(warm, warm_near, warm_arrived)
    warm_copy.start()

    @pl.loop(0, OUT_CHUNKS)
    def _(c):
        for copy in copies(c):
            copy.start()

    warm_copy.wait()

    def step(c, total):
        for copy in copies(c):
            copy.wait()
        part = block(c, wide)
        merged = merge(near[:, part], far_[:, part])
        merged_out[:, part] = merged
        return total + lax.dot_general(
            warm_near[:, part].astype(bf16),
            merged,
            (((1,), (1,)), ((), ())),
            preferred_element_type=f32,
        )

    total = lax.fori_loop(0, OUT_CHUNKS, step, jnp.zeros((8, near.shape[0]), f32))
    for d in range(16):
        for k in range(2):
            send[d, k] = total[:, k * LANES : (k + 1) * LANES]


def first_kv(core, grad, error, warm, merged_out, merged_kv, stored_out, keep, give, warm_near,
             near, far_, done, arrived, sent, warm_arrived, out_sent):
    rows = near.shape[0] // KV_CHUNKS

    def copies(c):
        part = block(c, rows)
        return [
            pltpu.make_async_copy(source.at[part], target.at[part], arrived.at[k, c])
            for k, (source, target) in enumerate(((grad, near), (error, far_)))
        ]

    def leaving(c):
        part = block(c, rows)
        return pltpu.make_async_copy(done.at[part], merged_kv.at[part], sent.at[c])

    warm_copy = pltpu.make_async_copy(warm, warm_near, warm_arrived)
    warm_copy.start()

    @pl.loop(0, KV_CHUNKS)
    def _(c):
        for copy in copies(c):
            copy.start()

    warm_copy.wait()
    out_copy = pltpu.make_async_copy(merged_out, stored_out, out_sent)
    out_copy.start()
    right = warm_near[...].astype(bf16)
    even = jnp.full((8, LANES), core[0], jnp.int32) == 0
    for c in range(KV_CHUNKS):
        for copy in copies(c):
            copy.wait()
        part = block(c, rows)
        merged = merge(near[part, :], far_[part, :])
        done[part, :] = merged
        leaving(c).start()
        sketch = lax.dot_general(
            right, merged, (((1,), (1,)), ((), ())), preferred_element_type=f32
        )
        for t in range(4):
            for k in range(2):
                first = (4 * t + k) * LANES
                zero = sketch[:, first : first + LANES]
                one = sketch[:, first + 2 * LANES : first + 3 * LANES]
                keep[4 * c + t, k] = jnp.where(even, zero, one)
                give[4 * c + t, k] = jnp.where(even, one, zero)

    out_copy.wait()

    @pl.loop(0, KV_CHUNKS)
    def _(c):
        leaving(c).wait()


def total_of(received, index):
    value = received[0, index]
    for d in range(1, received.shape[0]):
        value = value + received[d, index]
    return value


def half_factor(left, merged_out, half, target):
    wide = merged_out.shape[1] // 4
    for c in range(2):
        part = pl.ds(pl.multiple_of((2 * half + c) * wide, wide), wide)
        terms = jnp.dot(left, merged_out[:, part], preferred_element_type=f32)
        total = terms[:8] + (terms[8:16] + terms[16:24])
        for t in range(8):
            target[8 * c + t, 0] = total[:, t * LANES : (t + 1) * LANES]


def second_give(core, received, merged_out, give, sketch_out, terms):
    tiles = [total_of(received, k) for k in range(2)]
    sketch_out[0] = tiles[0]
    sketch_out[1] = tiles[1]
    value = jnp.concatenate(tiles, axis=1)
    high = value.astype(bf16)
    middle, low = split(value - high.astype(f32))
    left = jnp.concatenate(
        [part.astype(f32) for part in (high, middle, low, jnp.zeros_like(low))], axis=0
    ).astype(bf16)
    terms[...] = left
    half_factor(left, merged_out, 1 - core[0], give)


def second_keep(core, terms, merged_out, merged_kv, keep, same_kv):
    del merged_kv, same_kv
    half_factor(terms[...], merged_out, core[0], keep)


def third(received, send):
    tiles = [total_of(received, k) for k in range(3)]
    for z in range(8):
        for k in range(3):
            send[z, k] = tiles[k]


def fourth(received, send):
    tiles = [total_of(received, k) for k in range(3)]
    for t in range(16):
        for k in range(3):
            send[t, k] = tiles[k]


def in_order(core, mine, other):
    even = jnp.full((8, LANES), core[0], jnp.int32) == 0
    tiles = []
    for t in range(16):
        for k in range(2):
            tiles.append(jnp.where(even, mine[t, k], other[t, k]))
        for k in range(2):
            tiles.append(jnp.where(even, other[t, k], mine[t, k]))
    return tiles


def partial_factor(core, which, tiles, merged_kv):
    base = lax.rem(core[0] + which, 2) * 256
    term = jnp.zeros((16, LANES), f32)
    for t in range(16):
        high, low = split(jnp.concatenate([tiles[t, 0], tiles[t, 1]], axis=1))
        left = jnp.concatenate([high.astype(f32), low.astype(f32)], axis=0).astype(bf16)
        rows = pl.ds(pl.multiple_of(t * 512 + base, 256), 256)
        term = term + jnp.dot(left, merged_kv[rows, :], preferred_element_type=f32)
    return term[:8] + term[8:]


def fifth_mine(core, mine, merged_kv, term):
    term[...] = partial_factor(core, 0, mine, merged_kv)


def fifth_other(core, other, merged_kv, begun, send):
    term = begun[...] + partial_factor(core, 1, other, merged_kv)
    for d in range(16):
        send[d] = term


def orthonormal_kv(core, mine, other, basis, lower, scale):
    tiles = in_order(core, mine, other)
    steps, inverse = cholesky(gram_columns(tiles))
    for j in range(8):
        lower[j] = steps[j]
    scale[...] = inverse
    for k, tile in enumerate(tiles):
        basis[:, k * LANES : (k + 1) * LANES] = substitute(tile, steps, inverse)


def finish_out(core, mine, other, warm, sketch_out, merged_out, factor, residual, basis_kv, lower_kv,
               scale_kv, near, done, factor_near, warm_near, arrived, sent, factor_sent,
               warm_arrived):
    wide = done.shape[1] // 4

    def arriving(c):
        part = block(c, wide)
        return pltpu.make_async_copy(merged_out.at[:, part], near.at[:, part], arrived.at[c])

    def leaving(c):
        part = block(c, wide)
        return pltpu.make_async_copy(done.at[:, part], residual.at[:, part], sent.at[c])

    warm_copy = pltpu.make_async_copy(warm, warm_near, warm_arrived)
    warm_copy.start()

    @pl.loop(0, 4)
    def _(c):
        arriving(c).start()

    even = jnp.full((8, LANES), core[0], jnp.int32) == 0
    values = [jnp.where(even, mine[t, 2], other[t, 2]) for t in range(16)]
    values += [jnp.where(even, other[t, 2], mine[t, 2]) for t in range(16)]
    warm_copy.wait()
    sums = [jnp.zeros((8, LANES), f32)] * 8
    for k, tile in enumerate(values):
        right = warm_near[:, k * LANES : (k + 1) * LANES].astype(bf16).astype(f32)
        for j in range(8):
            sums[j] = sums[j] + right * row(tile, j)
    steps, scale = cholesky(
        [jnp.broadcast_to(jnp.sum(total, axis=1, keepdims=True), (8, LANES)) for total in sums]
    )
    basis = [substitute(sketch_out[k], steps, scale) for k in range(2)]
    left = left_terms(jnp.concatenate(basis, axis=1))
    values = [substitute(tile, steps, scale) * (1.0 / 16.0) for tile in values]
    for k, value in enumerate(values):
        factor_near[:, k * LANES : (k + 1) * LANES] = value
    factor_copy = pltpu.make_async_copy(factor_near, factor, factor_sent)
    factor_copy.start()
    for c in range(4):
        right = right_terms(jnp.concatenate(values[8 * c : 8 * c + 8], axis=1))
        part = block(c, wide)
        approx = jnp.dot(left, right, preferred_element_type=f32)
        arriving(c).wait()
        done[:, part] = (near[:, part].astype(f32) - approx).astype(bf16)
        leaving(c).start()

    orthonormal_kv(core, mine, other, basis_kv, lower_kv, scale_kv)

    @pl.loop(0, 4)
    def _(c):
        leaving(c).wait()

    factor_copy.wait()


def finish_kv(received, lower, scale, basis, merged_kv, factor, residual, done, factor_near, sent,
              factor_sent):
    rows = 1024

    def leaving(c):
        part = block(c, rows)
        return pltpu.make_async_copy(done.at[part], residual.at[part], sent.at[c])

    value = received[0]
    for d in range(1, 16):
        value = value + received[d]
    value = substitute(value, [lower[j] for j in range(8)], scale[...]) * (1.0 / 16.0)
    factor_near[...] = value
    factor_copy = pltpu.make_async_copy(factor_near, factor, factor_sent)
    factor_copy.start()
    right = right_terms(value)
    for c in range(8):
        part = block(c, rows)
        left = left_terms(basis[:, part])
        approx = jnp.dot(left, right, preferred_element_type=f32)
        done[part, :] = (merged_kv[part, :].astype(f32) - approx).astype(bf16)
        leaving(c).start()

    @pl.loop(0, 8)
    def _(c):
        leaving(c).wait()

    factor_copy.wait()


def exchange(value, axis, groups=None):
    return lax.all_to_all(value, axis, 0, 0, axis_index_groups=groups)


def call(kernel, outs, ins, args, scratch=(), seconds=1.0, aliases=None):
    return pl.pallas_call(
        kernel,
        out_shape=outs,
        in_specs=ins,
        out_specs=jax.tree.map(
            lambda out: far if isinstance(out, pl.MemoryRef) and out.memory_space == pltpu.HBM else whole,
            outs,
            is_leaf=lambda out: not isinstance(out, tuple),
        ),
        scratch_shapes=list(scratch),
        input_output_aliases=aliases or {},
        compiler_params=limit,
        cost_estimate=pl.CostEstimate(
            flops=0, bytes_accessed=int(seconds * 2_000_000), transcendentals=0
        ),
        name=kernel.__name__,
    )(*args)


far = pl.BlockSpec(memory_space=pltpu.HBM)
scalar = pl.BlockSpec(memory_space=pltpu.SMEM)


def per_device(grad_kv, error_kv, grad_out, error_out, warm_kv, warm_out):
    grad_kv, error_kv, grad_out, error_out = (
        distant(value[0]) for value in (grad_kv, error_kv, grad_out, error_out)
    )
    kv_shape, out_shape = grad_kv.shape, grad_out.shape
    columns = [[2 * z + c for z in [6, 7, 5, 4, 3, 2, 1, 0]] for c in range(2)]
    replicas = [[13, 15, 14, 12, 11, 10, 9, 8, 7, 6, 5, 4, 3, 2, 1, 0]]
    swap = [(d, d ^ 1) for d in range(16)]
    other_way = [10, 15, 14, 13, 12, 11, 9, 8, 7, 6, 5, 4, 3, 2, 1, 0]
    planes = [
        [(2 * z + c) * 16 + other_way[t] for t in range(16)]
        for z in range(8)
        for c in range(2)
    ]
    core = (lax.axis_index("dp") % 2).astype(jnp.int32).reshape(1)

    def tiles(*lead):
        return pltpu.VMEM((*lead, 8, LANES), f32)

    merged_out, send = call(
        first_out,
        (pltpu.VMEM(out_shape, bf16), tiles(16, 2)),
        [far] * 3,
        (grad_out, error_out, distant(warm_out.T)),
        [
            pltpu.VMEM((8, out_shape[1]), f32),
            pltpu.VMEM(out_shape, bf16),
            pltpu.VMEM(out_shape, bf16),
            pltpu.SemaphoreType.DMA((2, OUT_CHUNKS)),
            pltpu.SemaphoreType.DMA,
        ],
        2.6,
    )
    received = exchange(send, "dp", replicas)
    merged_kv, stored, keep_kv, give_kv = call(
        first_kv,
        (pltpu.HBM(kv_shape, bf16), pltpu.HBM(out_shape, bf16), tiles(16, 2), tiles(16, 2)),
        [scalar] + [far] * 3 + [whole],
        (core, grad_kv, error_kv, distant(warm_kv.T), resident(merged_out)),
        [
            pltpu.VMEM((8, kv_shape[1]), f32),
            pltpu.VMEM(kv_shape, bf16),
            pltpu.VMEM(kv_shape, bf16),
            pltpu.VMEM(kv_shape, bf16),
            pltpu.SemaphoreType.DMA((2, KV_CHUNKS)),
            pltpu.SemaphoreType.DMA((KV_CHUNKS,)),
            pltpu.SemaphoreType.DMA,
            pltpu.SemaphoreType.DMA,
        ],
        2.6,
    )
    give_out, sketch_out, terms = call(
        second_give,
        (tiles(16, 1), tiles(2), pltpu.VMEM((32, out_shape[0]), bf16)),
        [scalar] + [whole] * 2,
        (core, resident(received), resident(merged_out)),
        seconds=0.3,
    )
    keep_out, merged_kv = call(
        second_keep,
        (tiles(16, 1), pltpu.HBM(kv_shape, bf16)),
        [scalar] + [whole] * 2 + [far],
        (core, resident(terms), resident(merged_out), distant(merged_kv)),
        seconds=0.2,
        aliases={3: 1},
    )
    kv = keep_kv + lax.ppermute(give_kv, "dp", swap)
    out = keep_out + lax.ppermute(give_out, "dp", swap)
    received = exchange(jnp.concatenate([kv, out], axis=1), ("dp", "tensor"), planes)
    send = call(third, tiles(8, 3), [whole], (resident(received),), seconds=0.1)
    received = exchange(send, "dp", columns)
    send = call(fourth, tiles(16, 3), [whole], (resident(received),), seconds=0.1)
    mine = exchange(send, ("dp", "tensor"), planes)
    other = lax.ppermute(mine, "dp", swap)
    begun = call(
        fifth_mine,
        tiles(),
        [scalar] + [whole] * 2,
        (core, resident(mine), resident(merged_kv)),
        seconds=0.5,
    )
    send = call(
        fifth_other,
        tiles(16),
        [scalar] + [whole] * 3,
        (core, resident(other), resident(merged_kv), resident(begun)),
        seconds=0.5,
    )
    received = exchange(send, "dp", replicas)
    factor_out, residual_out, basis, lower, scale = call(
        finish_out,
        (
            pltpu.HBM((8, out_shape[1]), f32),
            pltpu.HBM(out_shape, bf16),
            pltpu.VMEM((8, kv_shape[0]), f32),
            tiles(8),
            tiles(),
        ),
        [scalar] + [whole] * 2 + [far, whole, far],
        (
            core,
            resident(mine),
            resident(other),
            distant(warm_out.T),
            resident(sketch_out),
            distant(stored),
        ),
        [
            pltpu.VMEM(out_shape, bf16),
            pltpu.VMEM(out_shape, bf16),
            pltpu.VMEM((8, out_shape[1]), f32),
            pltpu.VMEM((8, out_shape[1]), f32),
            pltpu.SemaphoreType.DMA((4,)),
            pltpu.SemaphoreType.DMA((4,)),
            pltpu.SemaphoreType.DMA,
            pltpu.SemaphoreType.DMA,
        ],
        2.5,
    )
    factor_kv, residual_kv = call(
        finish_kv,
        (pltpu.HBM((8, kv_shape[1]), f32), pltpu.HBM(kv_shape, bf16)),
        [whole] * 5,
        tuple(resident(value) for value in (received, lower, scale, basis, merged_kv)),
        [
            pltpu.VMEM(kv_shape, bf16),
            pltpu.VMEM((8, kv_shape[1]), f32),
            pltpu.SemaphoreType.DMA((8,)),
            pltpu.SemaphoreType.DMA,
        ],
        2.5,
    )
    return factor_kv.T, factor_out.T, residual_kv[None], residual_out[None]


def solution(mesh):
    placed = (
        P("dp", None, "tensor"),
        P("dp", None, "tensor"),
        P("dp", "tensor", None),
        P("dp", "tensor", None),
        P("tensor", None),
        P(),
    )
    return jax.shard_map(
        per_device,
        mesh=mesh,
        in_specs=placed,
        out_specs=(P("tensor", None), P(), P("dp", None, "tensor"), P("dp", "tensor", None)),
        check_vma=False,
    )
```
